512 devices in a mesh: gx: 16 (over z, core), gy: 8 (over y), gz: 4 (over x).
Axes of the slice: x: 4, y: 8, z: 8, core: 2. Of those that a mesh axis runs over, the one named last changes fastest.
Arguments:
- source: float32 [32, 128, 1024], P('gz', 'gx', 'gy'), may hold values from -24 to 24
- decay_rate: float32 [32, 128, 1024], P('gz', 'gx', 'gy'), may hold values from 0.005 to 1
- dispersion: float32 [3, 32, 128, 1024], P(None, 'gz', 'gx', 'gy'), may hold values from 0.1 to 2
- velocity: float32 [3, 32, 128, 1024], P(None, 'gz', 'gx', 'gy'), may hold values from 0.1 to 2
- upwind: int32 [3, 32, 128, 1024], P(None, 'gz', 'gx', 'gy'), may hold values 0 or 1
Outputs:
- adjoint: float32 [32, 128, 1024], P('gz', 'gx', 'gy')
The draws below stay inside these ranges and needn't reach their ends.
All inputs are finite; a program needn't handle non-finite values. No bound on the sum of `upwind` on one device may be relied on, other than what follows from the above.
Results may differ from the reference program's by a relative error of at most 0.0008.
Values sent between devices are 32-bit elements; how exact they have to be, the bound alone decides.
A program may use at most 128 MiB of HBM per device.

```python
import math
import jax
import jax.numpy as jnp
from jax import lax

LEVELS = 3
SWEEPS = 2
COARSE_SWEEPS = 8
NZ = 32
NX = 128
NY = 1024


def draw_source(key, part):
    key = jax.random.fold_in(key, 11)
    return 4.0 * jax.random.truncated_normal(key, -5.0, 5.0, (NZ, NX, NY), jnp.float32)


def with_ends(values, key, smallest, high):
    place = [jax.random.randint(jax.random.fold_in(key, axis), (), 0, length) for axis, length in enumerate(values.shape)]
    widest = values.shape.index(max(values.shape))
    neighbour = place[:widest] + [(place[widest] + 1) % values.shape[widest]] + place[widest + 1:]
    return values.at[tuple(place)].set(smallest).at[tuple(neighbour)].set(high)


def block_scale(rng, extent, pieces, low, high):
    level, own = 1.0, jax.random.fold_in(rng, 6)
    for position, shards_of in pieces:
        draws = jnp.exp(jax.random.uniform(jax.random.fold_in(own, position), (shards_of,), jnp.float32, low / len(pieces), high / len(pieces)))
        level = level * jnp.repeat(draws, extent[position] // shards_of).reshape([-1 if axis == position else 1 for axis in range(len(extent))])
    return level


def setup_inputs(seed: int = 0) -> dict:
    keys = jax.random.split(jax.random.key(seed), 6)
    return {
        "source": draw_source(jax.random.fold_in(keys[5], 71), 0),
        "decay_rate": jnp.clip(jnp.exp(math.log(1.0) - 5.2983174 * jax.random.uniform(keys[1], (NZ, NX, NY), jnp.float32) ** block_scale(keys[1], (NZ, NX, NY), ((0, 4), (1, 16), (2, 8)), -0.2, 0.2)), 0.005, 1.0),
        "dispersion": jnp.clip(jnp.exp(math.log(2.0) - 2.9957323 * jax.random.uniform(keys[2], (3, NZ, NX, NY), jnp.float32) ** block_scale(keys[2], (3, NZ, NX, NY), ((1, 4), (2, 16), (3, 8)), -0.2, 0.2)), 0.1, 2.0),
        "velocity": jnp.clip(jnp.exp(math.log(2.0) - 2.9957323 * jax.random.uniform(keys[3], (3, NZ, NX, NY), jnp.float32) ** block_scale(keys[3], (3, NZ, NX, NY), ((1, 4), (2, 16), (3, 8)), -0.2, 0.2)), 0.1, 2.0),
        "upwind": with_ends((jax.random.randint(keys[4], (3, NZ, NX, NY), 0, 2) < 1).astype(jnp.int32), jax.random.fold_in(keys[4], 1), 0, 1),
    }


relax_weight = 0.7


def restrict_sum(values):
    dims = values.shape
    blocks = values.reshape(dims[0] // 2, 2, dims[1] // 2, 2, dims[2] // 2, 2)
    return blocks.sum(axis=(1, 3, 5))


def coarse_faces(values, direction, pick):
    dims = values.shape
    blocks = values.reshape(dims[0] // 2, 2, dims[1] // 2, 2, dims[2] // 2, 2)
    chosen = lax.slice_in_dim(blocks, pick, pick + 1, axis=2 * direction + 1)
    return chosen.sum(axis=(1, 3, 5))


def prolong_copy(coarse):
    dims = coarse.shape
    wide = jnp.broadcast_to(coarse[:, None, :, None, :, None], (dims[0], 2, dims[1], 2, dims[2], 2))
    return wide.reshape(2 * dims[0], 2 * dims[1], 2 * dims[2])


def apply_operator(values, padded, rates, upper_terms, lower_terms):
    nexts = (padded[2:, 1:-1, 1:-1], padded[1:-1, 2:, 1:-1], padded[1:-1, 1:-1, 2:])
    prevs = (padded[:-2, 1:-1, 1:-1], padded[1:-1, :-2, 1:-1], padded[1:-1, 1:-1, :-2])
    result = rates * values
    for direction in range(3):
        result = result + upper_terms[direction] * (values - nexts[direction]) + lower_terms[direction] * (values - prevs[direction])
    return result


def diagonal_of(rates, upper_terms, lower_terms):
    total = rates
    for direction in range(3):
        total = total + upper_terms[direction] + lower_terms[direction]
    return total


def face_pair(k_ext, v_ext, f_ext, direction, positions, total):
    length = k_ext.shape[direction] - 2

    def part(array, begin):
        return lax.slice_in_dim(array, begin, begin + length, axis=direction)

    k_prev, k_here, k_next = part(k_ext, 0), part(k_ext, 1), part(k_ext, 2)
    v_prev, v_here, v_next = part(v_ext, 0), part(v_ext, 1), part(v_ext, 2)
    f_prev, f_here = part(f_ext, 0), part(f_ext, 1)
    upper = jnp.where(positions == total - 1, 0.0, 0.5 * (k_here + k_next) + f_here * (0.5 * (v_here + v_next)))
    lower = jnp.where(positions == 0, 0.0, 0.5 * (k_prev + k_here) + (1.0 - f_prev) * (0.5 * (v_prev + v_here)))
    return upper, lower


def build_levels(rates, uppers, lowers):
    levels = []
    for depth in range(LEVELS + 1):
        levels.append((rates, uppers, lowers, diagonal_of(rates, uppers, lowers)))
        if depth < LEVELS:
            rates = restrict_sum(rates)
            uppers = [coarse_faces(uppers[direction], direction, 1) for direction in range(3)]
            lowers = [coarse_faces(lowers[direction], direction, 0) for direction in range(3)]
    return levels


def sweeps(rhs, level, start, steps_count, neighbours):
    rates, upper_terms, lower_terms, diagonal = level
    current = start
    for step in range(steps_count):
        if current is None:
            current = relax_weight * rhs / diagonal
        else:
            image = apply_operator(current, neighbours(current), rates, upper_terms, lower_terms)
            current = current + relax_weight * (rhs - image) / diagonal
    return current


def cycle(rhs, levels, depth, neighbours, coarsest):
    if depth == len(levels) - 1:
        return coarsest(rhs)
    level = levels[depth]
    current = sweeps(rhs, level, None, SWEEPS, neighbours)
    residual = rhs - apply_operator(current, neighbours(current), level[0], level[1], level[2])
    correction = cycle(restrict_sum(residual), levels, depth + 1, neighbours, coarsest)
    current = current + prolong_copy(correction)
    return sweeps(rhs, level, current, SWEEPS, neighbours)


def local_rim(values):
    return jnp.pad(values, 1)


def reference(source, decay_rate, dispersion, velocity, upwind):
    flags = upwind.astype(jnp.float32)
    uppers, lowers = [], []
    for direction in range(3):
        widths = [(0, 0), (0, 0), (0, 0)]
        widths[direction] = (1, 1)
        positions = lax.broadcasted_iota(jnp.int32, source.shape, direction)
        upper, lower = face_pair(jnp.pad(dispersion[direction], widths), jnp.pad(velocity[direction], widths), jnp.pad(flags[direction], widths), direction, positions, source.shape[direction])
        uppers.append(upper)
        lowers.append(lower)
    levels = build_levels(decay_rate, uppers, lowers)

    def coarsest(rhs):
        return sweeps(rhs, levels[LEVELS], None, COARSE_SWEEPS, local_rim)

    return cycle(source, levels, 0, local_rim, coarsest)
```

```python
import jax
import jax.numpy as jnp
from jax import lax
from jax.experimental import pallas as pl
from jax.experimental.pallas import tpu as pltpu
from jax.sharding import PartitionSpec as P

MESH = pl.DeviceIdType.MESH
SIZES = (("gz", 4), ("gx", 16), ("gy", 8))
F32 = jnp.float32
RELAX = 0.7
KEEP = 1.0 - RELAX

ZX = [(k, a) for k in range(4) for a in (0, 1, -1) if (k, a) != (0, 0)]


def at(offset):
    return {
        name: lax.rem(lax.axis_index(name) + (step + size), size)
        for (name, size), step in zip(SIZES, offset)
    }


class Net:
    def __init__(self, send_sems, recv_sems):
        self.send_sems, self.recv_sems, self.copies = send_sems, recv_sems, []

    def send(self, src, dst, offset):
        index = len(self.copies)
        copy = pltpu.make_async_remote_copy(
            src_ref=src,
            dst_ref=dst,
            send_sem=self.send_sems.at[index],
            recv_sem=self.recv_sems.at[index],
            device_id=at(offset),
            device_id_type=MESH,
        )
        copy.start()
        self.copies.append(copy)
        return copy


def wait(copies):
    for copy in copies:
        copy.wait_recv()


def iota(shape, dim):
    return lax.broadcasted_iota(jnp.int32, shape, dim)


def mat(rows, cols, where):
    return jnp.where(where(iota((rows, cols), 0), iota((rows, cols), 1)), 1.0, 0.0).astype(F32)


def dot(a, b):
    return jnp.dot(a, b, preferred_element_type=F32, precision=lax.Precision.HIGHEST)


def roll(x, shift, axis):
    size = x.shape[axis]
    shift = shift % size
    return pltpu.roll(x, shift, axis) if shift else x


def low_lanes(i, parity):
    if parity is None:
        return i >= 0
    return (i & 1) == parity


PICKS = ((1, None, None), (0, None, None), (None, 1, None), (None, 0, None), (None, None, 1), (None, None, 0), (None, None, None))


def kernel(
    src_ref, r_ref, k_ref, v_ref, f_ref, out_ref,
    e0a, e0z, e0y, xb0, zlo, zhi, ylo, yhi,
    ea, ex, ey, exy, pk, pkr,
    cu, d0, va, vx, vy,
    wa, wx, wpk, wpkr,
    ys, ylr, yhr, c1, c2, c3,
    b1c, b1r, b1l, b1h, b1, v1p, v1q,
    b2c, b2r, b2l, b2h, b2, v2p, v2q,
    b3, go_a, go_b, ssem, rsem,
):
    net = Net(ssem, rsem)
    send = net.send
    gz, gx, gy = lax.axis_index("gz"), lax.axis_index("gx"), lax.axis_index("gy")
    sx, ly = iota((8, 128), 0), iota((8, 128), 1)

    barrier = pltpu.get_barrier_semaphore()
    greeted = [(1, 0, 0), (2, 0, 0), (3, 0, 0), (0, 1, 0), (0, -1, 0), (0, 0, 1), (0, 0, -1)]
    for offset in greeted:
        pl.semaphore_signal(barrier, inc=1, device_id=at(offset), device_id_type=MESH)

    e0a[0] = k_ref[1]
    e0a[1] = v_ref[1]
    e0a[2] = f_ref[1].astype(F32)
    e0z[0] = k_ref[0, 7]
    e0z[1] = v_ref[0, 7]
    e0z[2] = f_ref[0, 7].astype(F32)
    e0z[3] = k_ref[0, 0]
    e0z[4] = v_ref[0, 0]
    packed = jnp.zeros((8, 128), F32)
    for f, ref in enumerate((k_ref, v_ref, f_ref)):
        for z in range(8):
            start = 16 * f + 2 * z
            moved = roll(ref[2, z].astype(F32), start + 1, 1)
            packed = jnp.where((ly >= start) & (ly < start + 2), moved, packed)
    e0y[...] = packed
    pl.semaphore_wait(barrier, len(greeted))
    e0 = [
        send(e0a.at[:, :, pl.ds(7, 1), :], xb0.at[:, :, pl.ds(7, 1), :], (0, 1, 0)),
        send(e0a.at[pl.ds(0, 2), :, pl.ds(0, 1), :], xb0.at[pl.ds(0, 2), :, pl.ds(0, 1), :], (0, -1, 0)),
        send(e0z.at[pl.ds(0, 3)], zlo, (1, 0, 0)),
        send(e0z.at[pl.ds(3, 2)], zhi, (-1, 0, 0)),
        send(e0y, ylo, (0, 0, 1)),
        send(e0y, yhi, (0, 0, -1)),
    ]

    def xprev(a, b):
        return roll(jnp.where(sx == 7, b, a), 1, 0)

    def xnext(a, b):
        return roll(jnp.where(sx == 0, b, a), -1, 0)

    def yprev(a, b):
        return roll(jnp.where(ly == 127, b, a), 1, 1)

    def ynext(a, b):
        return roll(jnp.where(ly == 0, b, a), -1, 1)

    wait(e0)
    for a in (2, -2):
        pl.semaphore_signal(go_a, inc=1, device_id=at((0, a, 0)), device_id_type=MESH)

    both0 = jnp.where((ly & 1) == 0, ylo[...], yhi[...])
    pack = jnp.zeros((8, 128), F32)
    for z in range(8):
        k, v = [k_ref[d, z] for d in range(3)], [v_ref[d, z] for d in range(3)]
        f = [f_ref[d, z].astype(F32) for d in range(3)]
        side = [roll(both0, -(16 * q + 2 * z + 1), 1) for q in range(3)]
        kn = [
            k_ref[0, z + 1] if z < 7 else zhi[0],
            xnext(k[1], xb0[0, z]),
            ynext(k[2], side[0]),
        ]
        vn = [
            v_ref[0, z + 1] if z < 7 else zhi[1],
            xnext(v[1], xb0[1, z]),
            ynext(v[2], side[1]),
        ]
        kp = [
            k_ref[0, z - 1] if z else zlo[0],
            xprev(k[1], xb0[0, z]),
            yprev(k[2], side[0]),
        ]
        vp = [
            v_ref[0, z - 1] if z else zlo[1],
            xprev(v[1], xb0[1, z]),
            yprev(v[2], side[1]),
        ]
        fp = [
            f_ref[0, z - 1].astype(F32) if z else zlo[2],
            xprev(f[1], xb0[2, z]),
            yprev(f[2], side[2]),
        ]
        last = [
            (gz == 3) if z == 7 else None,
            (sx == 7) & (gx == 15),
            (ly == 127) & (gy == 7),
        ]
        first = [
            (gz == 0) if z == 0 else None,
            (sx == 0) & (gx == 0),
            (ly == 0) & (gy == 0),
        ]
        terms = []
        for d in range(3):
            up = 0.5 * (k[d] + kn[d]) + f[d] * (0.5 * (v[d] + vn[d]))
            down = 0.5 * (kp[d] + k[d]) + (1.0 - fp[d]) * (0.5 * (vp[d] + v[d]))
            if last[d] is not None:
                up = jnp.where(last[d], 0.0, up)
            if first[d] is not None:
                down = jnp.where(first[d], 0.0, down)
            terms += [up, down]
        rate = r_ref[z]
        diag = rate
        for term in terms:
            diag = diag + term
        scale = RELAX / diag
        d0[z] = diag * (1.0 / RELAX)
        for q in range(6):
            cu[q, z] = terms[q]
            scaled = terms[q] * scale
            ea[1 + q, 2 + z] = scaled
            start = 32 + 16 * q + 2 * z
            pack = jnp.where((ly >= start) & (ly < start + 2), roll(scaled, start + 1, 1), pack)
        begun = src_ref[z] * scale
        ea[0, 2 + z] = begun
        pack = jnp.where((ly >= 4 * z) & (ly < 4 * z + 4), roll(begun, 4 * z + 2, 1), pack)
    pk[...] = pack

    diagonal_y = [(0, 0, 1), (0, 0, -1)] + [(s, 0, t) for s in (1, -1) for t in (1, -1)] + [(0, s, t) for s in (1, -1) for t in (1, -1)]

    def rim(a, x, p, pr):
        copies = []
        for s in (1, -1):
            mine, theirs = (8, 0) if s == 1 else (2, 10)
            copies.append(send(a.at[pl.ds(mine, 2)], a.at[pl.ds(theirs, 2)], (s, 0, 0)))
            row = 6 if s == 1 else 0
            copies.append(send(a.at[pl.ds(2, 8), pl.ds(row, 2)], x.at[pl.ds(1, 8), pl.ds(row, 2)], (0, s, 0)))
        for i, offset in enumerate(diagonal_y):
            copies.append(send(p, pr.at[i], offset))
        for s in (1, -1):
            for t in (1, -1):
                plane, row = (9 if s == 1 else 2), (7 if t == 1 else 0)
                copies.append(
                    send(a.at[pl.ds(plane, 1), pl.ds(row, 1)], x.at[pl.ds(0 if s == 1 else 9, 1), pl.ds(row, 1)], (s, t, 0))
                )
        return copies

    r1 = []
    for s in (1, -1):
        mine, theirs, row = (9, 1, 7) if s == 1 else (2, 10, 0)
        r1.append(send(ea.at[pl.ds(1, 6), pl.ds(mine, 1)], ea.at[pl.ds(1, 6), pl.ds(theirs, 1)], (s, 0, 0)))
        r1.append(
            send(ea.at[pl.ds(1, 6), pl.ds(2, 8), pl.ds(row, 1)], ex.at[pl.ds(1, 6), pl.ds(1, 8), pl.ds(row, 1)], (0, s, 0))
        )
    r1 += rim(ea.at[0], ex.at[0], pk, pkr)

    own1 = (iota((16, 128), 1) >= 32) & (iota((16, 128), 1) < 96)

    def scaled_terms(fields, inside):
        diag = fields[6]
        for q in range(6):
            diag = diag + fields[q]
        diag = jnp.where(inside, diag, 1.0)
        scale = jnp.where(inside, RELAX / diag, 0.0)
        return [fields[q] * scale for q in range(6)] + [jnp.where(inside, diag * (1.0 / RELAX), 0.0)]

    def pairs(q, a, b):
        pick = PICKS[q][0]
        return a + b if pick is None else (b if pick else a)

    def lanes01(pick):
        return mat(128, 128, lambda i, j: (j == 32 + (i >> 1)) & low_lanes(i, pick))

    def lanes12(pick):
        return mat(128, 128, lambda i, j: (j == 16 + (i >> 1)) & (i >= 32) & (i < 96) & low_lanes(i, pick))

    def lanes23(pick):
        return mat(128, 128, lambda i, j: (j == (i >> 1)) & (i >= 32) & (i < 64) & low_lanes(i, pick))

    def rows01(pick):
        return mat(16, 32, lambda i, j: ((j >> 3) == (i & 3)) & (((j & 7) >> 1) == (i >> 2)) & low_lanes(j, pick))

    def rows12(pz, px):
        return mat(
            8, 16,
            lambda i, j: ((j >> 3) == (i >> 1)) & (((j & 3) >> 1) == (i & 1)) & low_lanes(j, pz) & low_lanes(j >> 2, px),
        )

    def rows23(pz, px):
        return mat(8, 8, lambda i, j: (i == 0) & (j < 4) & low_lanes(j, pz) & low_lanes(j >> 1, px))

    level1 = []
    for q in range(7):
        planes = [pairs(q, (cu[q, 2 * z] if q < 6 else r_ref[2 * z]), (cu[q, 2 * z + 1] if q < 6 else r_ref[2 * z + 1])) for z in range(4)]
        stacked = jnp.concatenate(planes, axis=0)
        level1.append(dot(dot(rows01(PICKS[q][1]), stacked), lanes01(PICKS[q][2])))
    level2 = [dot(dot(rows12(PICKS[q][0], PICKS[q][1]), level1[q]), lanes12(PICKS[q][2])) for q in range(7)]
    level3 = [dot(dot(rows23(PICKS[q][0], PICKS[q][1]), level2[q]), lanes23(PICKS[q][2])) for q in range(7)]
    inside2 = (ly >= 32) & (ly < 64) & (sx < 4)
    inside3 = (ly >= 16) & (ly < 32) & (sx < 1)
    scaled1 = scaled_terms(level1, own1)
    scaled2 = scaled_terms(level2, inside2)
    scaled3 = scaled_terms(level3, inside3)
    for q in range(7):
        ys[pl.ds(16 * q, 16), :] = roll(scaled1[q], 64, 1)
        ys[pl.ds(112 + 8 * q, 8), :] = roll(scaled2[q], 32, 1) + roll(scaled2[q], -32, 1)
        ys[pl.ds(168 + 8 * q, 8), :] = roll(scaled3[q], 16, 1) + roll(scaled3[q], -16, 1)
    stage_y = [send(ys, ylr, (0, 0, 1)), send(ys, yhr, (0, 0, -1))]

    wait(stage_y)
    lane16 = iota((16, 128), 1)
    for q in range(7):
        part = pl.ds(16 * q, 16)
        merged = jnp.where(lane16 < 32, ylr[part, :], jnp.where(lane16 >= 96, yhr[part, :], scaled1[q]))
        for x in range(4):
            c1[q, 4 + x, 0:4, :] = merged[4 * x : 4 * x + 4]
        part = pl.ds(112 + 8 * q, 8)
        merged = jnp.where(ly < 32, ylr[part, :], jnp.where(ly >= 64, yhr[part, :], scaled2[q]))
        for x in range(2):
            c2[q, 6 + x, 0:2, :] = merged[2 * x : 2 * x + 2]
        part = pl.ds(168 + 8 * q, 8)
        merged = jnp.where(ly < 16, ylr[part, :], jnp.where(ly >= 32, yhr[part, :], scaled3[q]))
        c3[q, 0, 0:1, :] = merged[0:1]

    def zslot(k):
        return (4 - k) % 4

    def xplace(own, per, a):
        return own - per * a

    c1_copies = [
        send(c1.at[:, pl.ds(4, 4), pl.ds(0, 4)], c1.at[:, pl.ds(xplace(4, 4, a), 4), pl.ds(4 * zslot(k), 4)], (k, a, 0))
        for k, a in ZX
    ]
    z_copies = []
    for k in (1, 2, 3):
        z_copies.append(send(c2.at[:, pl.ds(6, 2), pl.ds(0, 2)], c2.at[:, pl.ds(6, 2), pl.ds(2 * zslot(k), 2)], (k, 0, 0)))
        z_copies.append(send(c3.at[:, pl.ds(0, 1), pl.ds(0, 1)], c3.at[:, pl.ds(0, 1), pl.ds(zslot(k), 1)], (k, 0, 0)))

    wait(r1)
    pl.semaphore_wait(go_a, 2)
    for a in (4, -4):
        pl.semaphore_signal(go_b, inc=1, device_id=at((0, a, 0)), device_id_type=MESH)

    def unpack(pr, y, xy):
        from_low = (ly & jnp.where(ly < 32, 2, 1)) == 0

        def both(low, high):
            return jnp.where(from_low, pr[low], pr[high])

        beside = both(0, 1)
        for z in range(8):
            y[1 + z] = roll(beside, -(4 * z + 2), 1)
        y[0] = roll(both(2, 3), -30, 1)
        y[9] = roll(both(4, 5), -2, 1)
        across = jnp.where(sx < 4, both(8, 9), both(6, 7))
        for z in range(8):
            xy[z] = roll(across, -(4 * z + 2), 1)
        return beside

    beside = unpack(pkr, ey.at[0], exy)
    for q in range(6):
        for z in range(8):
            ey[1 + q, 1 + z] = roll(beside, -(32 + 16 * q + 2 * z + 1), 1)

    def sweep(here, zp, zn, xp, xn, yp, yn, rhs, s):
        total = KEEP * here + rhs
        total = total + s[0] * zn + s[1] * zp
        total = total + s[2] * xn + s[3] * xp
        return total + s[4] * yn + s[5] * yp

    def sweep_a(a, x, y, p, outer):
        here = a[p]
        bx, by = x[p - outer], y[p - outer]
        return sweep(
            here, a[p - 1], a[p + 1], xprev(here, bx), xnext(here, bx), yprev(here, by), ynext(here, by),
            ea[0, p], [ea[1 + q, p] for q in range(6)],
        )

    def rim_sweep(a, x, y, xy):
        for p in range(1, 11):
            va[p] = sweep_a(a, x, y, p, 1)
        for z in range(8):
            here = x[1 + z]
            ba, bxy = a[2 + z], xy[z]
            vx[z] = sweep(
                here, x[z], x[2 + z], xprev(here, ba), xnext(here, ba), yprev(here, bxy), ynext(here, bxy),
                ex[0, 1 + z], [ex[1 + q, 1 + z] for q in range(6)],
            )
            here = y[1 + z]
            vy[z] = sweep(
                here, y[z], y[2 + z], xprev(here, bxy), xnext(here, bxy), yprev(here, ba), ynext(here, ba),
                ey[0, 1 + z], [ey[1 + q, 1 + z] for q in range(6)],
            )

    rim_sweep(ea.at[0], ex.at[0], ey.at[0], exy)
    planes = []
    for z in range(4):
        two = [(sweep_a(va, vx, vy, 2 + p, 2) - va[2 + p]) * d0[p] for p in (2 * z, 2 * z + 1)]
        planes.append(two[0] + two[1])
    rhs1 = dot(dot(rows01(None), jnp.concatenate(planes, axis=0)), lanes01(None))
    d1_own = jnp.concatenate([c1[6, 4 + x, 0:4, :] for x in range(4)], axis=0)
    rhs1 = jnp.where(own1, rhs1 / jnp.where(own1, d1_own, 1.0), 0.0)
    turned = roll(rhs1, 64, 1)
    for x in range(4):
        b1c[4 + x, 0:4, :] = rhs1[4 * x : 4 * x + 4]
        b1r[x, 0:4, :] = turned[4 * x : 4 * x + 4]

    r2 = []
    for k, a in ZX:
        there = (pl.ds(xplace(4, 4, a), 4), pl.ds(4 * zslot(k), 4))
        r2.append(send(b1c.at[pl.ds(4, 4), pl.ds(0, 4)], b1c.at[there], (k, a, 0)))
    for k, a in [(0, 0)] + ZX:
        there = (pl.ds(xplace(4, 4, a), 4), pl.ds(4 * zslot(k), 4))
        r2.append(send(b1r.at[:, pl.ds(0, 4)], b1l.at[there], (k, a, 1)))
        r2.append(send(b1r.at[:, pl.ds(0, 4)], b1h.at[there], (k, a, -1)))

    pack = jnp.zeros((8, 128), F32)
    for z in range(8):
        plane = va[2 + z]
        wa[2 + z] = plane
        pack = jnp.where((ly >= 4 * z) & (ly < 4 * z + 4), roll(plane, 4 * z + 2, 1), pack)
    wpk[...] = pack
    up0 = rim(wa, wx, wpk, wpkr)

    wait(z_copies)
    c2_copies = [
        send(c2.at[:, pl.ds(6, 2)], c2.at[:, pl.ds(xplace(6, 2, a), 2)], (0, a, 0)) for a in (1, -1, 2, -2, 3, -3)
    ]

    def sweep_l(v, b, c, x):
        here = v[x]
        return sweep(
            here, roll(here, 1, 0), roll(here, -1, 0), v[x - 1], v[x + 1], roll(here, 1, 1), roll(here, -1, 1),
            b[x], [c[q, x] for q in range(6)],
        )

    wait(c1_copies)
    wait(r2)
    for x in range(12):
        b1[x] = jnp.where(lane16 < 32, b1l[x], jnp.where(lane16 >= 96, b1h[x], b1c[x]))
    for x in range(1, 11):
        v1p[x] = sweep_l(b1, b1, c1, x)
    rows = []
    for x in range(2):
        two = [(sweep_l(v1p, b1, c1, p) - v1p[p]) * c1[6, p] for p in (4 + 2 * x, 5 + 2 * x)]
        rows.append(two[0] + two[1])
    rows = dot(jnp.concatenate(rows, axis=0), lanes12(None))
    halve = mat(8, 16, lambda i, j: (j >> 1) == i)
    for x in range(2):
        inside = (ly >= 32) & (ly < 64)
        rhs2 = dot(halve, rows[16 * x : 16 * x + 16])
        rhs2 = jnp.where(inside, rhs2 / jnp.where(inside, c2[6, 6 + x], 1.0), 0.0)
        b2c[6 + x] = rhs2
        b2r[x] = roll(rhs2, 32, 1) + roll(rhs2, -32, 1)

    r3 = []
    for a in (0, 1, -1, 2, -2, 3, -3):
        there = pl.ds(xplace(6, 2, a), 2)
        if a:
            r3.append(send(b2c.at[pl.ds(6, 2)], b2c.at[there], (0, a, 0)))
        r3.append(send(b2r, b2l.at[there], (0, a, 1)))
        r3.append(send(b2r, b2h.at[there], (0, a, -1)))
    pl.semaphore_wait(go_b, 2)
    c3_copies = [
        send(c3.at[pl.ds(0, 6), pl.ds(0, 1), pl.ds(0, 4)], c3.at[pl.ds(0, 6), pl.ds(16 - a, 1), pl.ds(0, 4)], (0, a, 0))
        for a in range(1, 16)
    ]

    wait(c2_copies)
    wait(r3)
    for x in range(14):
        b2[x] = jnp.where(ly < 32, b2l[x], jnp.where(ly >= 64, b2h[x], b2c[x]))
    for x in range(2, 12):
        v2p[x] = sweep_l(b2, b2, c2, x)
    two = [(sweep_l(v2p, b2, c2, p) - v2p[p]) * c2[6, p] for p in (6, 7)]
    rows = dot(two[0] + two[1], mat(128, 128, lambda i, j: (j == (i >> 1)) & (i < 96)))
    rhs3 = dot(mat(8, 8, lambda i, j: (j >> 1) == (i & 3)), rows)

    def twice(block):
        return jnp.where(sx < 4, block, roll(block, 4, 0))

    inside = ly < 48
    rhs3 = jnp.where(inside, rhs3 / jnp.where(inside, twice(c3[6, 0]), 1.0), 0.0)
    b3[0] = rhs3

    r4 = [send(b3.at[pl.ds(0, 1)], b3.at[pl.ds(16 - a, 1)], (0, a, 0)) for a in range(1, 16)]
    wait(c3_copies)
    terms3 = [[twice(c3[q, x]) for x in range(16)] for q in range(6)]
    wait(r4)
    rhs3 = [b3[x] for x in range(16)]
    here = rhs3
    for _ in range(7):
        here = [
            sweep(
                here[x], roll(here[x], 1, 0), roll(here[x], -1, 0), here[(x + 15) % 16], here[(x + 1) % 16],
                roll(here[x], 1, 1), roll(here[x], -1, 1), rhs3[x], [terms3[q][x] for q in range(6)],
            )
            for x in range(16)
        ]

    wide = dot(mat(8, 8, lambda i, j: j == (i >> 1)), jnp.concatenate([here[(X + 16) % 16] for X in range(-2, 3)], axis=1))
    wide = jnp.concatenate([wide[:, 128 * i : 128 * i + 128] for i in range(5)], axis=0)
    wide = dot(wide, mat(128, 128, lambda i, j: (i == (j >> 1)) & (j < 96)))
    for x in range(2, 12):
        i = (x >> 1) - 1
        v2p[x] = v2p[x] + wide[8 * i : 8 * i + 8]
    for x in range(3, 11):
        v2q[x] = sweep_l(v2p, b2, c2, x)
    ups = [sweep_l(v2q, b2, c2, x) for x in range(4, 10)]

    wide = dot(jnp.concatenate(ups, axis=0), mat(128, 128, lambda i, j: i == 16 + (j >> 1)))
    wide = dot(mat(16, 8, lambda i, j: j == (i >> 1)), jnp.concatenate([wide[8 * i : 8 * i + 8] for i in range(6)], axis=1))
    for x in range(1, 11):
        i = x >> 1
        v1p[x] = v1p[x] + wide[:, 128 * i : 128 * i + 128]
    for x in range(2, 10):
        v1q[x] = sweep_l(v1p, b1, c1, x)
    ups = [sweep_l(v1q, b1, c1, x) for x in range(3, 9)]

    def lanes10(i, j):
        main = (j < 128) & (i == 32 + (j >> 1))
        return main | ((j >= 254) & (i == 31)) | ((j >= 128) & (j < 130) & (i == 96))

    def rows10(i, j):
        xi, zr = j >> 4, j & 15
        main = (i < 96) & (zr == (((i >> 4) + 15) & 15)) & (xi == 1 + ((i & 7) >> 1))
        n = i - 96
        beside = (i >= 96) & (zr == ((((n >> 3) + 31) >> 1) & 15)) & (
            (((n & 7) >= 6) & (xi == 0)) | (((n & 7) < 2) & (xi == 5))
        )
        return main | beside

    wide = dot(jnp.concatenate(ups, axis=0), mat(128, 256, lanes10))
    wide = dot(mat(176, 96, rows10), wide)
    wait(up0)
    low = (ly & 2) == 0
    beside = jnp.where(low, wpkr[0], wpkr[1])
    low_z = jnp.where(low, wpkr[2], wpkr[3])
    high_z = jnp.where(low, wpkr[4], wpkr[5])
    across = jnp.where(sx < 4, jnp.where(low, wpkr[8], wpkr[9]), jnp.where(low, wpkr[6], wpkr[7]))
    a = [wa[p] + wide[8 * p : 8 * p + 8, 0:128] for p in range(12)]
    x = [wx[p] + wide[96 + 8 * p : 104 + 8 * p, 0:128] for p in range(10)]
    y = []
    for p in range(10):
        if p == 0:
            base = roll(low_z, -30, 1)
        elif p == 9:
            base = roll(high_z, -2, 1)
        else:
            base = roll(beside, -(4 * (p - 1) + 2), 1)
        y.append(base + wide[8 * (p + 1) : 8 * (p + 1) + 8, 128:256])
    xy = [roll(across, -(4 * z + 2), 1) + wide[104 + 8 * z : 112 + 8 * z, 128:256] for z in range(8)]
    rim_sweep(a, x, y, xy)
    for z in range(8):
        out_ref[z] = sweep_a(va, vx, vy, 2 + z, 2)
    for copy in net.copies:
        copy.wait_send()


def on_device(source, decay_rate, dispersion, velocity, upwind):
    def vmem(*shape):
        return pltpu.VMEM(shape, F32)

    tile = (8, 128)
    scratch = [
        vmem(3, 8, *tile), vmem(5, *tile), vmem(*tile), vmem(3, 8, *tile), vmem(3, *tile), vmem(2, *tile), vmem(*tile), vmem(*tile),
        vmem(7, 12, *tile), vmem(7, 10, *tile), vmem(7, 10, *tile), vmem(8, *tile), vmem(*tile), vmem(10, *tile),
        vmem(6, 8, *tile), vmem(8, *tile), vmem(12, *tile), vmem(8, *tile), vmem(8, *tile),
        vmem(12, *tile), vmem(10, *tile), vmem(*tile), vmem(10, *tile),
        vmem(224, 128), vmem(224, 128), vmem(224, 128), vmem(7, 12, 16, 128), vmem(7, 14, *tile), vmem(7, 16, *tile),
        vmem(12, 16, 128), vmem(4, *tile), vmem(12, 16, 128), vmem(12, 16, 128), vmem(12, 16, 128), vmem(12, 16, 128), vmem(12, 16, 128),
        vmem(14, *tile), vmem(2, *tile), vmem(14, *tile), vmem(14, *tile), vmem(14, *tile), vmem(14, *tile), vmem(14, *tile),
        vmem(16, *tile),
        pltpu.SemaphoreType.REGULAR, pltpu.SemaphoreType.REGULAR,
        pltpu.SemaphoreType.DMA((160,)), pltpu.SemaphoreType.DMA((160,)),
    ]
    return pl.pallas_call(
        kernel,
        out_shape=jax.ShapeDtypeStruct((8, 8, 128), F32),
        in_specs=[pl.BlockSpec(memory_space=pltpu.VMEM)] * 5,
        out_specs=pl.BlockSpec(memory_space=pltpu.VMEM),
        scratch_shapes=scratch,
        compiler_params=pltpu.CompilerParams(
            collective_id=0, has_side_effects=True, vmem_limit_bytes=32 * 1024 * 1024
        ),
    )(source, decay_rate, dispersion, velocity, upwind)


def solution(mesh):
    field, vector = P("gz", "gx", "gy"), P(None, "gz", "gx", "gy")
    return jax.shard_map(
        on_device, mesh=mesh, in_specs=(field, field, vector, vector, vector), out_specs=field, check_vma=False
    )
```

```python
import jax
import jax.numpy as jnp
from jax import lax
from jax.experimental import pallas as pl
from jax.experimental.pallas import tpu as pltpu
from jax.sharding import PartitionSpec as P

MESH = pl.DeviceIdType.MESH
SIZES = (("gz", 4), ("gx", 16), ("gy", 8))
F32 = jnp.float32
RELAX = 0.7
KEEP = 1.0 - RELAX
COPIES = 208

ZX = [(k, a) for k in range(4) for a in (0, 1, -1) if (k, a) != (0, 0)]


def at(offset):
    return {
        name: lax.rem(lax.axis_index(name) + (step + size), size)
        for (name, size), step in zip(SIZES, offset)
    }


class Net:
    def __init__(self, send_sems, recv_sems):
        self.send_sems, self.recv_sems, self.copies = send_sems, recv_sems, []

    def send(self, src, dst, offset):
        index = len(self.copies)
        copy = pltpu.make_async_remote_copy(
            src_ref=src,
            dst_ref=dst,
            send_sem=self.send_sems.at[index],
            recv_sem=self.recv_sems.at[index],
            device_id=at(offset),
            device_id_type=MESH,
        )
        copy.start()
        self.copies.append(copy)
        return copy


def wait(copies):
    for copy in copies:
        copy.wait_recv()


def iota(shape, dim):
    return lax.broadcasted_iota(jnp.int32, shape, dim)


def mat(rows, cols, where):
    return jnp.where(where(iota((rows, cols), 0), iota((rows, cols), 1)), 1.0, 0.0).astype(F32)


def dot(a, b):
    return jnp.dot(a, b, preferred_element_type=F32, precision=lax.Precision.HIGHEST)


def roll(x, shift, axis):
    size = x.shape[axis]
    shift = shift % size
    return pltpu.roll(x, shift, axis) if shift else x


def low_lanes(i, parity):
    if parity is None:
        return i >= 0
    return (i & 1) == parity


PICKS = ((1, None, None), (0, None, None), (None, 1, None), (None, 0, None), (None, None, 1), (None, None, 0), (None, None, None))


def kernel(
    src_hbm, r_hbm, k_hbm, v_hbm, f_hbm, out_ref,
    src_ref, r_ref, k_ref, v_ref, f_ref, in_sems,
    e0a, e0z, e0y, xb0, zlo, zhi, ylo, yhi,
    ea, ex, ey, exy, pk, pkr,
    cu, d0, va, vx, vy,
    wa, wx, wpk, wpkr,
    p1, s1, s1l, s1h, a2, a3, c1, c2, c3,
    b1c, b1, v1p, v1q,
    b2c, b2r, b2l, b2h, b2, v2p, v2q,
    b3, go_a, go_b, go_c, ssem, rsem,
):
    net = Net(ssem, rsem)
    send = net.send
    gz, gx, gy = lax.axis_index("gz"), lax.axis_index("gx"), lax.axis_index("gy")
    sx, ly = iota((8, 128), 0), iota((8, 128), 1)

    fetches = [
        pltpu.make_async_copy(here, there, in_sems.at[i])
        for i, (here, there) in enumerate(
            ((k_hbm, k_ref), (v_hbm, v_ref), (f_hbm, f_ref), (src_hbm, src_ref), (r_hbm, r_ref))
        )
    ]
    for fetch in fetches:
        fetch.start()
    barrier = pltpu.get_barrier_semaphore()
    greeted = [(1, 0, 0), (2, 0, 0), (3, 0, 0), (0, 1, 0), (0, -1, 0), (0, 0, 1), (0, 0, -1)]
    for offset in greeted:
        pl.semaphore_signal(barrier, inc=1, device_id=at(offset), device_id_type=MESH)

    for fetch in fetches[:3]:
        fetch.wait()
    e0a[0] = k_ref[1]
    e0a[1] = v_ref[1]
    e0a[2] = f_ref[1].astype(F32)
    e0z[0] = k_ref[0, 7]
    e0z[1] = v_ref[0, 7]
    e0z[2] = f_ref[0, 7].astype(F32)
    e0z[3] = k_ref[0, 0]
    e0z[4] = v_ref[0, 0]
    packed = jnp.zeros((8, 128), F32)
    for f, ref in enumerate((k_ref, v_ref, f_ref)):
        for z in range(8):
            start = 16 * f + 2 * z
            moved = roll(ref[2, z].astype(F32), start + 1, 1)
            packed = jnp.where((ly >= start) & (ly < start + 2), moved, packed)
    e0y[...] = packed
    pl.semaphore_wait(barrier, len(greeted))
    e0 = [
        send(e0a.at[:, :, pl.ds(7, 1), :], xb0.at[:, :, pl.ds(7, 1), :], (0, 1, 0)),
        send(e0a.at[pl.ds(0, 2), :, pl.ds(0, 1), :], xb0.at[pl.ds(0, 2), :, pl.ds(0, 1), :], (0, -1, 0)),
        send(e0z.at[pl.ds(0, 3)], zlo, (1, 0, 0)),
        send(e0z.at[pl.ds(3, 2)], zhi, (-1, 0, 0)),
        send(e0y, ylo, (0, 0, 1)),
        send(e0y, yhi, (0, 0, -1)),
    ]

    def xprev(a, b):
        return roll(jnp.where(sx == 7, b, a), 1, 0)

    def xnext(a, b):
        return roll(jnp.where(sx == 0, b, a), -1, 0)

    def yprev(a, b):
        return roll(jnp.where(ly == 127, b, a), 1, 1)

    def ynext(a, b):
        return roll(jnp.where(ly == 0, b, a), -1, 1)

    wait(e0)
    for a in (2, -2):
        pl.semaphore_signal(go_a, inc=1, device_id=at((0, a, 0)), device_id_type=MESH)
    for t in (1, -1):
        pl.semaphore_signal(go_c, inc=1, device_id=at((0, 0, t)), device_id_type=MESH)
    for fetch in fetches[3:]:
        fetch.wait()

    both0 = jnp.where((ly & 1) == 0, ylo[...], yhi[...])
    pack = jnp.zeros((8, 128), F32)
    for z in range(8):
        k, v = [k_ref[d, z] for d in range(3)], [v_ref[d, z] for d in range(3)]
        f = [f_ref[d, z].astype(F32) for d in range(3)]
        side = [roll(both0, -(16 * q + 2 * z + 1), 1) for q in range(3)]
        kn = [
            k_ref[0, z + 1] if z < 7 else zhi[0],
            xnext(k[1], xb0[0, z]),
            ynext(k[2], side[0]),
        ]
        vn = [
            v_ref[0, z + 1] if z < 7 else zhi[1],
            xnext(v[1], xb0[1, z]),
            ynext(v[2], side[1]),
        ]
        kp = [
            k_ref[0, z - 1] if z else zlo[0],
            xprev(k[1], xb0[0, z]),
            yprev(k[2], side[0]),
        ]
        vp = [
            v_ref[0, z - 1] if z else zlo[1],
            xprev(v[1], xb0[1, z]),
            yprev(v[2], side[1]),
        ]
        fp = [
            f_ref[0, z - 1].astype(F32) if z else zlo[2],
            xprev(f[1], xb0[2, z]),
            yprev(f[2], side[2]),
        ]
        last = [
            (gz == 3) if z == 7 else None,
            (sx == 7) & (gx == 15),
            (ly == 127) & (gy == 7),
        ]
        first = [
            (gz == 0) if z == 0 else None,
            (sx == 0) & (gx == 0),
            (ly == 0) & (gy == 0),
        ]
        terms = []
        for d in range(3):
            up = 0.5 * (k[d] + kn[d]) + f[d] * (0.5 * (v[d] + vn[d]))
            down = 0.5 * (kp[d] + k[d]) + (1.0 - fp[d]) * (0.5 * (vp[d] + v[d]))
            if last[d] is not None:
                up = jnp.where(last[d], 0.0, up)
            if first[d] is not None:
                down = jnp.where(first[d], 0.0, down)
            terms += [up, down]
        rate = r_ref[z]
        diag = rate
        for term in terms:
            diag = diag + term
        scale = RELAX / diag
        d0[z] = diag * (1.0 / RELAX)
        for q in range(6):
            cu[q, z] = terms[q]
            scaled = terms[q] * scale
            ea[1 + q, 2 + z] = scaled
            start = 32 + 16 * q + 2 * z
            pack = jnp.where((ly >= start) & (ly < start + 2), roll(scaled, start + 1, 1), pack)
        begun = src_ref[z] * scale
        ea[0, 2 + z] = begun
        pack = jnp.where((ly >= 4 * z) & (ly < 4 * z + 4), roll(begun, 4 * z + 2, 1), pack)
    pk[...] = pack

    diagonal_y = [(0, 0, 1), (0, 0, -1)] + [(s, 0, t) for s in (1, -1) for t in (1, -1)] + [(0, s, t) for s in (1, -1) for t in (1, -1)]

    def rim(a, x, p, pr):
        copies = []
        for s in (1, -1):
            mine, theirs = (8, 0) if s == 1 else (2, 10)
            copies.append(send(a.at[pl.ds(mine, 2)], a.at[pl.ds(theirs, 2)], (s, 0, 0)))
            row = 6 if s == 1 else 0
            copies.append(send(a.at[pl.ds(2, 8), pl.ds(row, 2)], x.at[pl.ds(1, 8), pl.ds(row, 2)], (0, s, 0)))
        for i, offset in enumerate(diagonal_y):
            copies.append(send(p, pr.at[i], offset))
        for s in (1, -1):
            for t in (1, -1):
                plane, row = (9 if s == 1 else 2), (7 if t == 1 else 0)
                copies.append(
                    send(a.at[pl.ds(plane, 1), pl.ds(row, 1)], x.at[pl.ds(0 if s == 1 else 9, 1), pl.ds(row, 1)], (s, t, 0))
                )
        return copies

    r1 = []
    for s in (1, -1):
        mine, theirs, row = (9, 1, 7) if s == 1 else (2, 10, 0)
        r1.append(send(ea.at[pl.ds(1, 6), pl.ds(mine, 1)], ea.at[pl.ds(1, 6), pl.ds(theirs, 1)], (s, 0, 0)))
        r1.append(
            send(ea.at[pl.ds(1, 6), pl.ds(2, 8), pl.ds(row, 1)], ex.at[pl.ds(1, 6), pl.ds(1, 8), pl.ds(row, 1)], (0, s, 0))
        )
    r1 += rim(ea.at[0], ex.at[0], pk, pkr)

    own1 = (iota((16, 128), 1) >= 32) & (iota((16, 128), 1) < 96)

    def scaled_terms(fields, inside):
        diag = fields[6]
        for q in range(6):
            diag = diag + fields[q]
        diag = jnp.where(inside, diag, 1.0)
        scale = jnp.where(inside, RELAX / diag, 0.0)
        return [fields[q] * scale for q in range(6)] + [jnp.where(inside, diag * (1.0 / RELAX), 0.0)]

    def pairs(q, a, b):
        pick = PICKS[q][0]
        return a + b if pick is None else (b if pick else a)

    def lanes01(pick):
        return mat(128, 128, lambda i, j: (j == 32 + (i >> 1)) & low_lanes(i, pick))

    def lanes12(pick):
        return mat(128, 128, lambda i, j: (j == 16 + (i >> 1)) & (i >= 32) & (i < 96) & low_lanes(i, pick))

    def lanes23(pick):
        return mat(128, 128, lambda i, j: (j == (i >> 1)) & (i >= 32) & (i < 64) & low_lanes(i, pick))

    def rows01(pick):
        return mat(16, 32, lambda i, j: ((j >> 3) == (i & 3)) & (((j & 7) >> 1) == (i >> 2)) & low_lanes(j, pick))

    def rows12(pz, px):
        return mat(
            8, 16,
            lambda i, j: ((j >> 3) == (i >> 1)) & (((j & 3) >> 1) == (i & 1)) & low_lanes(j, pz) & low_lanes(j >> 2, px),
        )

    def rows23(pz, px):
        return mat(8, 8, lambda i, j: (i == 0) & (j < 4) & low_lanes(j, pz) & low_lanes(j >> 1, px))

    def halves(block):
        return jnp.where(own8, block[0:8], roll(block[8:16], 64, 1))

    def zslot(k):
        return (4 - k) % 4

    def xplace(own, per, a):
        return own - per * a

    own8 = (ly >= 32) & (ly < 96)
    level1 = []
    for q in range(7):
        planes = [pairs(q, (cu[q, 2 * z] if q < 6 else r_ref[2 * z]), (cu[q, 2 * z + 1] if q < 6 else r_ref[2 * z + 1])) for z in range(4)]
        stacked = jnp.concatenate(planes, axis=0)
        level1.append(dot(dot(rows01(PICKS[q][1]), stacked), lanes01(PICKS[q][2])))
    scaled1 = scaled_terms(level1, own1)
    d1_own = scaled1[6]
    strip = jnp.zeros((8, 128), F32)
    for q in range(7):
        block = halves(scaled1[q])
        for x in range(2):
            p1[q, 1, x, 0:4, :] = block[4 * x : 4 * x + 4]
        if q < 6:
            for h in range(2):
                t = 4 * (2 * q + h)
                moved = roll(scaled1[q][8 * h : 8 * h + 8], t - 92, 1)
                strip = jnp.where(((ly >= t) & (ly < t + 4)) | ((ly >= t + 68) & (ly < t + 72)), moved, strip)
    for x in range(2):
        s1[x, 0:4, :] = strip[4 * x : 4 * x + 4]
    c1_copies = []
    for k, a in ZX:
        n = 6 if a else 7
        c1_copies.append(
            send(
                p1.at[pl.ds(0, n), pl.ds(1, 1), :, pl.ds(0, 4)],
                p1.at[pl.ds(0, n), pl.ds(1 - a, 1), :, pl.ds(4 * zslot(k), 4)],
                (k, a, 0),
            )
        )
    pl.semaphore_wait(go_c, 2)
    for k, a in [(0, 0)] + ZX:
        for t in (1, -1):
            there = s1l if t == 1 else s1h
            c1_copies.append(send(s1.at[:, pl.ds(0, 4)], there.at[1 - a, :, pl.ds(4 * zslot(k), 4)], (k, a, t)))

    level2 = [dot(dot(rows12(PICKS[q][0], PICKS[q][1]), level1[q]), lanes12(PICKS[q][2])) for q in range(7)]
    level3 = [dot(dot(rows23(PICKS[q][0], PICKS[q][1]), level2[q]), lanes23(PICKS[q][2])) for q in range(7)]
    inside2 = (ly >= 32) & (ly < 64) & (sx < 4)
    inside3 = (ly >= 16) & (ly < 32) & (sx < 1)
    scaled2 = scaled_terms(level2, inside2)
    scaled3 = scaled_terms(level3, inside3)
    group = [jnp.zeros((8, 128), F32), jnp.zeros((8, 128), F32)]
    line = jnp.zeros((8, 128), F32)
    for q in range(7):
        g, j = q // 4, q % 4
        group[g] = group[g] + roll(scaled2[q], 32 * j - 32, 1)
        line = line + roll(scaled3[q], 16 * q - 16, 1)
    for g in range(2):
        for x in range(2):
            a2[1, 2 * g + x, 0:2, :] = group[g][2 * x : 2 * x + 2]
    a3[1, 0:1, :] = line[0:1]
    z_copies = []
    for k in range(4):
        for t in (0, 1, -1):
            if k or t:
                z_copies.append(
                    send(a2.at[pl.ds(1, 1), :, pl.ds(0, 2)], a2.at[pl.ds(1 - t, 1), :, pl.ds(2 * zslot(k), 2)], (k, 0, t))
                )
                z_copies.append(send(a3.at[pl.ds(1, 1), pl.ds(0, 1)], a3.at[pl.ds(1 - t, 1), pl.ds(zslot(k), 1)], (k, 0, t)))

    wait(r1)
    pl.semaphore_wait(go_a, 2)
    for a in (4, -4):
        pl.semaphore_signal(go_b, inc=1, device_id=at((0, a, 0)), device_id_type=MESH)

    def unpack(pr, y, xy):
        from_low = (ly & jnp.where(ly < 32, 2, 1)) == 0

        def both(low, high):
            return jnp.where(from_low, pr[low], pr[high])

        beside = both(0, 1)
        for z in range(8):
            y[1 + z] = roll(beside, -(4 * z + 2), 1)
        y[0] = roll(both(2, 3), -30, 1)
        y[9] = roll(both(4, 5), -2, 1)
        across = jnp.where(sx < 4, both(8, 9), both(6, 7))
        for z in range(8):
            xy[z] = roll(across, -(4 * z + 2), 1)
        return beside

    beside = unpack(pkr, ey.at[0], exy)
    for q in range(6):
        for z in range(8):
            ey[1 + q, 1 + z] = roll(beside, -(32 + 16 * q + 2 * z + 1), 1)

    def sweep(here, zp, zn, xp, xn, yp, yn, rhs, s):
        total = KEEP * here + rhs
        total = total + s[0] * zn + s[1] * zp
        total = total + s[2] * xn + s[3] * xp
        return total + s[4] * yn + s[5] * yp

    def sweep_a(a, x, y, p, outer):
        here = a[p]
        bx, by = x[p - outer], y[p - outer]
        return sweep(
            here, a[p - 1], a[p + 1], xprev(here, bx), xnext(here, bx), yprev(here, by), ynext(here, by),
            ea[0, p], [ea[1 + q, p] for q in range(6)],
        )

    def rim_sweep(a, x, y, xy):
        for p in range(1, 11):
            va[p] = sweep_a(a, x, y, p, 1)
        for z in range(8):
            here = x[1 + z]
            ba, bxy = a[2 + z], xy[z]
            vx[z] = sweep(
                here, x[z], x[2 + z], xprev(here, ba), xnext(here, ba), yprev(here, bxy), ynext(here, bxy),
                ex[0, 1 + z], [ex[1 + q, 1 + z] for q in range(6)],
            )
            here = y[1 + z]
            vy[z] = sweep(
                here, y[z], y[2 + z], xprev(here, bxy), xnext(here, bxy), yprev(here, ba), ynext(here, ba),
                ey[0, 1 + z], [ey[1 + q, 1 + z] for q in range(6)],
            )

    rim_sweep(ea.at[0], ex.at[0], ey.at[0], exy)
    planes = []
    for z in range(4):
        two = [(sweep_a(va, vx, vy, 2 + p, 2) - va[2 + p]) * d0[p] for p in (2 * z, 2 * z + 1)]
        planes.append(two[0] + two[1])
    rhs1 = dot(dot(rows01(None), jnp.concatenate(planes, axis=0)), lanes01(None))
    rhs1 = halves(jnp.where(own1, rhs1 / jnp.where(own1, d1_own, 1.0), 0.0))
    for x in range(2):
        b1c[1, 1, x, 0:4, :] = rhs1[4 * x : 4 * x + 4]

    r2 = []
    for t in (0, 1, -1):
        for k, a in [(0, 0)] + ZX:
            if (k, a, t) != (0, 0, 0):
                r2.append(
                    send(b1c.at[1, 1, :, pl.ds(0, 4)], b1c.at[1 - t, 1 - a, :, pl.ds(4 * zslot(k), 4)], (k, a, t))
                )

    pack = jnp.zeros((8, 128), F32)
    for z in range(8):
        plane = va[2 + z]
        wa[2 + z] = plane
        pack = jnp.where((ly >= 4 * z) & (ly < 4 * z + 4), roll(plane, 4 * z + 2, 1), pack)
    wpk[...] = pack
    up0 = rim(wa, wx, wpk, wpkr)

    wait(z_copies)
    for q in range(7):
        g, j = q // 4, q % 4
        for x in range(2):
            low, mid, high = [roll(a2[t, 2 * g + x], 32 * t - 32 * j, 1) for t in range(3)]
            c2[q, 6 + x] = jnp.where(ly < 32, low, jnp.where(ly < 64, mid, jnp.where(ly < 96, high, 0.0)))
    c2_copies = [
        send(c2.at[pl.ds(0, 6), pl.ds(6, 2)], c2.at[pl.ds(0, 6), pl.ds(xplace(6, 2, a), 2)], (0, a, 0))
        for a in (1, -1, 2, -2, 3, -3)
    ]
    fields3 = []
    for q in range(7):
        low, mid, high = [roll(a3[t], 16 * t - 16 * q, 1) for t in range(3)]
        fields3.append(jnp.where(ly < 16, low, jnp.where(ly < 32, mid, jnp.where(ly < 48, high, 0.0))))
    for q in range(3):
        c3[q, 0] = jnp.where(ly < 64, fields3[2 * q], roll(fields3[2 * q + 1], 64, 1))

    def sweep_l(v, b, c, x):
        here = v[x]
        return sweep(
            here, roll(here, 1, 0), roll(here, -1, 0), v[x - 1], v[x + 1], roll(here, 1, 1), roll(here, -1, 1),
            b[x], [c[q, x] for q in range(6)],
        )

    wait(c1_copies)
    lane16 = iota((16, 128), 1)
    own16 = (lane16 >= 32) & (lane16 < 96)
    for i in range(3):
        for x in range(2):
            rims = jnp.where(lane16 < 64, s1l[i, x], s1h[i, x])
            for q in range(6):
                block = p1[q, i, x]
                c1[q, 4 * i + x] = jnp.where(own16, block, roll(rims, 28 - 8 * q, 1))
                c1[q, 4 * i + 2 + x] = jnp.where(own16, roll(block, 64, 1), roll(rims, 24 - 8 * q, 1))
    for x in range(2):
        block = p1[6, 1, x]
        c1[6, 4 + x] = block
        c1[6, 6 + x] = roll(block, 64, 1)
    wait(r2)
    for i in range(3):
        for x in range(2):
            low, mid, high = [b1c[t, i, x] for t in range(3)]
            b1[4 * i + x] = jnp.where(own16, mid, roll(jnp.where(lane16 >= 64, low, high), 64, 1))
            b1[4 * i + 2 + x] = jnp.where(own16, roll(mid, 64, 1), jnp.where(lane16 < 64, low, high))
    for x in range(1, 11):
        v1p[x] = sweep_l(b1, b1, c1, x)
    rows = []
    for x in range(2):
        two = [(sweep_l(v1p, b1, c1, p) - v1p[p]) * c1[6, p] for p in (4 + 2 * x, 5 + 2 * x)]
        rows.append(two[0] + two[1])
    rows = dot(jnp.concatenate(rows, axis=0), lanes12(None))
    halve = mat(8, 16, lambda i, j: (j >> 1) == i)
    for x in range(2):
        inside = (ly >= 32) & (ly < 64)
        rhs2 = dot(halve, rows[16 * x : 16 * x + 16])
        rhs2 = jnp.where(inside, rhs2 / jnp.where(inside, c2[6, 6 + x], 1.0), 0.0)
        b2c[6 + x] = rhs2
        b2r[x] = roll(rhs2, 32, 1) + roll(rhs2, -32, 1)

    r3 = []
    for a in (0, 1, -1, 2, -2, 3, -3):
        there = pl.ds(xplace(6, 2, a), 2)
        if a:
            r3.append(send(b2c.at[pl.ds(6, 2)], b2c.at[there], (0, a, 0)))
        r3.append(send(b2r, b2l.at[there], (0, a, 1)))
        r3.append(send(b2r, b2h.at[there], (0, a, -1)))
    pl.semaphore_wait(go_b, 2)
    c3_copies = [
        send(c3.at[:, pl.ds(0, 1), pl.ds(0, 4)], c3.at[:, pl.ds(16 - a, 1), pl.ds(0, 4)], (0, a, 0))
        for a in range(1, 16)
    ]

    wait(c2_copies)
    wait(r3)
    for x in range(14):
        b2[x] = jnp.where(ly < 32, b2l[x], jnp.where(ly >= 64, b2h[x], b2c[x]))
    for x in range(2, 12):
        v2p[x] = sweep_l(b2, b2, c2, x)
    two = [(sweep_l(v2p, b2, c2, p) - v2p[p]) * c2[6, p] for p in (6, 7)]
    rows = dot(two[0] + two[1], mat(128, 128, lambda i, j: (j == (i >> 1)) & (i < 96)))
    rhs3 = dot(mat(8, 8, lambda i, j: (j >> 1) == (i & 3)), rows)

    def twice(block):
        return jnp.where(sx < 4, block, roll(block, 4, 0))

    inside = ly < 48
    rhs3 = jnp.where(inside, rhs3 / jnp.where(inside, twice(fields3[6]), 1.0), 0.0)
    b3[0] = rhs3

    r4 = [send(b3.at[pl.ds(0, 1)], b3.at[pl.ds(16 - a, 1)], (0, a, 0)) for a in range(1, 16)]
    wait(c3_copies)
    terms3 = []
    for q in range(3):
        terms3.append([twice(c3[q, x]) for x in range(16)])
        terms3.append([roll(block, 64, 1) for block in terms3[-1]])
    wait(r4)
    rhs3 = [b3[x] for x in range(16)]
    here = rhs3
    for _ in range(7):
        here = [
            sweep(
                here[x], roll(here[x], 1, 0), roll(here[x], -1, 0), here[(x + 15) % 16], here[(x + 1) % 16],
                roll(here[x], 1, 1), roll(here[x], -1, 1), rhs3[x], [terms3[q][x] for q in range(6)],
            )
            for x in range(16)
        ]

    wide = dot(mat(8, 8, lambda i, j: j == (i >> 1)), jnp.concatenate([here[(X + 16) % 16] for X in range(-2, 3)], axis=1))
    wide = jnp.concatenate([wide[:, 128 * i : 128 * i + 128] for i in range(5)], axis=0)
    wide = dot(wide, mat(128, 128, lambda i, j: (i == (j >> 1)) & (j < 96)))
    for x in range(2, 12):
        i = (x >> 1) - 1
        v2p[x] = v2p[x] + wide[8 * i : 8 * i + 8]
    for x in range(3, 11):
        v2q[x] = sweep_l(v2p, b2, c2, x)
    ups = [sweep_l(v2q, b2, c2, x) for x in range(4, 10)]

    wide = dot(jnp.concatenate(ups, axis=0), mat(128, 128, lambda i, j: i == 16 + (j >> 1)))
    wide = dot(mat(16, 8, lambda i, j: j == (i >> 1)), jnp.concatenate([wide[8 * i : 8 * i + 8] for i in range(6)], axis=1))
    for x in range(1, 11):
        i = x >> 1
        v1p[x] = v1p[x] + wide[:, 128 * i : 128 * i + 128]
    for x in range(2, 10):
        v1q[x] = sweep_l(v1p, b1, c1, x)
    ups = [sweep_l(v1q, b1, c1, x) for x in range(3, 9)]

    def lanes10(i, j):
        main = (j < 128) & (i == 32 + (j >> 1))
        return main | ((j >= 254) & (i == 31)) | ((j >= 128) & (j < 130) & (i == 96))

    def rows10(i, j):
        xi, zr = j >> 4, j & 15
        main = (i < 96) & (zr == (((i >> 4) + 15) & 15)) & (xi == 1 + ((i & 7) >> 1))
        n = i - 96
        beside = (i >= 96) & (zr == ((((n >> 3) + 31) >> 1) & 15)) & (
            (((n & 7) >= 6) & (xi == 0)) | (((n & 7) < 2) & (xi == 5))
        )
        return main | beside

    wide = dot(jnp.concatenate(ups, axis=0), mat(128, 256, lanes10))
    wide = dot(mat(176, 96, rows10), wide)
    wait(up0)
    low = (ly & 2) == 0
    beside = jnp.where(low, wpkr[0], wpkr[1])
    low_z = jnp.where(low, wpkr[2], wpkr[3])
    high_z = jnp.where(low, wpkr[4], wpkr[5])
    across = jnp.where(sx < 4, jnp.where(low, wpkr[8], wpkr[9]), jnp.where(low, wpkr[6], wpkr[7]))
    a = [wa[p] + wide[8 * p : 8 * p + 8, 0:128] for p in range(12)]
    x = [wx[p] + wide[96 + 8 * p : 104 + 8 * p, 0:128] for p in range(10)]
    y = []
    for p in range(10):
        if p == 0:
            base = roll(low_z, -30, 1)
        elif p == 9:
            base = roll(high_z, -2, 1)
        else:
            base = roll(beside, -(4 * (p - 1) + 2), 1)
        y.append(base + wide[8 * (p + 1) : 8 * (p + 1) + 8, 128:256])
    xy = [roll(across, -(4 * z + 2), 1) + wide[104 + 8 * z : 112 + 8 * z, 128:256] for z in range(8)]
    rim_sweep(a, x, y, xy)
    for z in range(8):
        out_ref[z] = sweep_a(va, vx, vy, 2 + z, 2)
    for copy in net.copies:
        copy.wait_send()


def on_device(source, decay_rate, dispersion, velocity, upwind):
    def vmem(*shape):
        return pltpu.VMEM(shape, F32)

    tile = (8, 128)
    scratch = [
        vmem(8, *tile), vmem(8, *tile), vmem(3, 8, *tile), vmem(3, 8, *tile), pltpu.VMEM((3, 8, *tile), jnp.int32),
        pltpu.SemaphoreType.DMA((5,)),
        vmem(3, 8, *tile), vmem(5, *tile), vmem(*tile), vmem(3, 8, *tile), vmem(3, *tile), vmem(2, *tile), vmem(*tile), vmem(*tile),
        vmem(7, 12, *tile), vmem(7, 10, *tile), vmem(7, 10, *tile), vmem(8, *tile), vmem(*tile), vmem(10, *tile),
        vmem(6, 8, *tile), vmem(8, *tile), vmem(12, *tile), vmem(8, *tile), vmem(8, *tile),
        vmem(12, *tile), vmem(10, *tile), vmem(*tile), vmem(10, *tile),
        vmem(7, 3, 2, 16, 128), vmem(2, *tile), vmem(3, 2, 16, 128), vmem(3, 2, 16, 128), vmem(3, 4, *tile), vmem(3, *tile),
        vmem(7, 12, 16, 128), vmem(7, 14, *tile), vmem(3, 16, *tile),
        vmem(3, 3, 2, 16, 128), vmem(12, 16, 128), vmem(12, 16, 128), vmem(12, 16, 128),
        vmem(14, *tile), vmem(2, *tile), vmem(14, *tile), vmem(14, *tile), vmem(14, *tile), vmem(14, *tile), vmem(14, *tile),
        vmem(16, *tile),
        pltpu.SemaphoreType.REGULAR, pltpu.SemaphoreType.REGULAR, pltpu.SemaphoreType.REGULAR,
        pltpu.SemaphoreType.DMA((COPIES,)), pltpu.SemaphoreType.DMA((COPIES,)),
    ]
    return pl.pallas_call(
        kernel,
        out_shape=jax.ShapeDtypeStruct((8, 8, 128), F32),
        in_specs=[pl.BlockSpec(memory_space=pltpu.HBM)] * 5,
        out_specs=pl.BlockSpec(memory_space=pltpu.VMEM),
        scratch_shapes=scratch,
        compiler_params=pltpu.CompilerParams(
            collective_id=0, has_side_effects=True, vmem_limit_bytes=32 * 1024 * 1024
        ),
    )(source, decay_rate, dispersion, velocity, upwind)


def solution(mesh):
    field, vector = P("gz", "gx", "gy"), P(None, "gz", "gx", "gy")
    return jax.shard_map(
        on_device, mesh=mesh, in_specs=(field, field, vector, vector, vector), out_specs=field, check_vma=False
    )
```

```python
import jax
import jax.numpy as jnp
from jax import lax
from jax.experimental import pallas as pl
from jax.experimental.pallas import tpu as pltpu
from jax.sharding import PartitionSpec as P

MESH = pl.DeviceIdType.MESH
SIZES = (("gz", 4), ("gx", 16), ("gy", 8))
F32 = jnp.float32
RELAX = 0.7
KEEP = 1.0 - RELAX
GROUPS = 10

ZX = [(k, a) for k in range(4) for a in (0, 1, -1) if (k, a) != (0, 0)]


class Net:
    def __init__(self, tally, send_sems, recv_sems):
        self.tally, self.send_sems, self.recv_sems = tally, send_sems, recv_sems
        self.rows, self.places = [], {}
        for name, size in SIZES:
            here = lax.axis_index(name)
            for step in range(size):
                self.places[name, step] = (here + step) & (size - 1) if step else here

    def at(self, offset):
        return {name: self.places[name, step % size] for (name, size), step in zip(SIZES, offset)}

    def signal(self, sem, offset):
        pl.semaphore_signal(sem, inc=1, device_id=self.at(offset), device_id_type=MESH)

    def group(self):
        self.rows.append(0)
        return len(self.rows) - 1

    def send(self, group, src, dst, offset):
        size = 1
        for n in src.shape:
            size *= n
        self.rows[group] += size // 128
        pltpu.make_async_remote_copy(
            src_ref=src,
            dst_ref=dst,
            send_sem=self.send_sems.at[group],
            recv_sem=self.recv_sems.at[group],
            device_id=self.at(offset),
            device_id_type=MESH,
        ).start()

    def whole(self, group):
        part = self.tally.at[pl.ds(0, self.rows[group])]
        return pltpu.make_async_remote_copy(
            src_ref=part,
            dst_ref=part,
            send_sem=self.send_sems.at[group],
            recv_sem=self.recv_sems.at[group],
            device_id=self.at((0, 0, 1)),
            device_id_type=MESH,
        )

    def wait(self, group):
        self.whole(group).wait_recv()

    def finish(self):
        for group in range(len(self.rows)):
            self.whole(group).wait_send()


def iota(shape, dim):
    return lax.broadcasted_iota(jnp.int32, shape, dim)


def mat(rows, cols, where):
    return jnp.where(where(iota((rows, cols), 0), iota((rows, cols), 1)), 1.0, 0.0).astype(F32)


def split(x):
    high = x.astype(jnp.bfloat16)
    return high, (x - high.astype(F32)).astype(jnp.bfloat16)


def dot(a, b, ones):
    if ones:
        b = b.astype(jnp.bfloat16)
        pairs = [(part, b) for part in split(a)]
    else:
        a = a.astype(jnp.bfloat16)
        pairs = [(a, part) for part in split(b)]
    high, low = [jnp.dot(x, y, preferred_element_type=F32) for x, y in pairs]
    return high + low


def left(a, b):
    return dot(a, b, 0)


def right(a, b):
    return dot(a, b, 1)


def roll(x, shift, axis):
    size = x.shape[axis]
    shift = shift % size
    return pltpu.roll(x, shift, axis) if shift else x


def low_lanes(i, parity):
    if parity is None:
        return i >= 0
    return (i & 1) == parity


PICKS = ((1, None, None), (0, None, None), (None, 1, None), (None, 0, None), (None, None, 1), (None, None, 0), (None, None, None))


def kernel(
    src_hbm, r_hbm, k_hbm, v_hbm, f_hbm, out_ref,
    src_ref, r_ref, k_ref, v_ref, f_ref, in_sems,
    e0a, e0z, e0y, xb0, zlo, zhi, ylo, yhi,
    ea, ex, ey, exy, pk, pkr,
    cu, d0, va, vx, vy,
    wa, wx, wpk, wpkr,
    p1, s1, s1l, s1h, a2, a3, c1, c2, c3,
    b1c, b1, v1p, v1q,
    b2c, b2r, b2l, b2h, b2, v2p, v2q,
    b3, go_a, go_b, go_c, tally, ssem, rsem,
):
    net = Net(tally, ssem, rsem)
    send, wait = net.send, net.wait
    gz, gx, gy = lax.axis_index("gz"), lax.axis_index("gx"), lax.axis_index("gy")
    sx, ly = iota((8, 128), 0), iota((8, 128), 1)

    fetches = [
        pltpu.make_async_copy(here, there, in_sems.at[i])
        for i, (here, there) in enumerate(
            ((k_hbm, k_ref), (v_hbm, v_ref), (f_hbm, f_ref), (src_hbm, src_ref), (r_hbm, r_ref))
        )
    ]
    for fetch in fetches:
        fetch.start()
    barrier = pltpu.get_barrier_semaphore()
    greeted = [(1, 0, 0), (2, 0, 0), (3, 0, 0), (0, 1, 0), (0, -1, 0), (0, 0, 1), (0, 0, -1)]
    for offset in greeted:
        net.signal(barrier, offset)

    for fetch in fetches[:3]:
        fetch.wait()
    e0a[0] = k_ref[1]
    e0a[1] = v_ref[1]
    e0a[2] = f_ref[1].astype(F32)
    e0z[0] = k_ref[0, 7]
    e0z[1] = v_ref[0, 7]
    e0z[2] = f_ref[0, 7].astype(F32)
    e0z[3] = k_ref[0, 0]
    e0z[4] = v_ref[0, 0]
    packed = jnp.zeros((8, 128), F32)
    for f, ref in enumerate((k_ref, v_ref, f_ref)):
        for z in range(8):
            start = 16 * f + 2 * z
            moved = roll(ref[2, z].astype(F32), start + 1, 1)
            packed = jnp.where((ly >= start) & (ly < start + 2), moved, packed)
    e0y[...] = packed
    pl.semaphore_wait(barrier, len(greeted))
    e0 = net.group()
    send(e0, e0a.at[:, :, pl.ds(7, 1), :], xb0.at[:, :, pl.ds(7, 1), :], (0, 1, 0))
    send(e0, e0a.at[pl.ds(0, 2), :, pl.ds(0, 1), :], xb0.at[pl.ds(0, 2), :, pl.ds(0, 1), :], (0, -1, 0))
    send(e0, e0z.at[pl.ds(0, 3)], zlo, (1, 0, 0))
    send(e0, e0z.at[pl.ds(3, 2)], zhi, (-1, 0, 0))
    send(e0, e0y, ylo, (0, 0, 1))
    send(e0, e0y, yhi, (0, 0, -1))

    def xprev(a, b):
        return roll(jnp.where(sx == 7, b, a), 1, 0)

    def xnext(a, b):
        return roll(jnp.where(sx == 0, b, a), -1, 0)

    def yprev(a, b):
        return roll(jnp.where(ly == 127, b, a), 1, 1)

    def ynext(a, b):
        return roll(jnp.where(ly == 0, b, a), -1, 1)

    wait(e0)
    for a in (2, -2):
        net.signal(go_a, (0, a, 0))
    for t in (1, -1):
        net.signal(go_c, (0, 0, t))
    for fetch in fetches[3:]:
        fetch.wait()

    both0 = jnp.where((ly & 1) == 0, ylo[...], yhi[...])
    pack = jnp.zeros((8, 128), F32)
    for z in range(8):
        k, v = [k_ref[d, z] for d in range(3)], [v_ref[d, z] for d in range(3)]
        f = [f_ref[d, z].astype(F32) for d in range(3)]
        side = [roll(both0, -(16 * q + 2 * z + 1), 1) for q in range(3)]
        kn = [
            k_ref[0, z + 1] if z < 7 else zhi[0],
            xnext(k[1], xb0[0, z]),
            ynext(k[2], side[0]),
        ]
        vn = [
            v_ref[0, z + 1] if z < 7 else zhi[1],
            xnext(v[1], xb0[1, z]),
            ynext(v[2], side[1]),
        ]
        kp = [
            k_ref[0, z - 1] if z else zlo[0],
            xprev(k[1], xb0[0, z]),
            yprev(k[2], side[0]),
        ]
        vp = [
            v_ref[0, z - 1] if z else zlo[1],
            xprev(v[1], xb0[1, z]),
            yprev(v[2], side[1]),
        ]
        fp = [
            f_ref[0, z - 1].astype(F32) if z else zlo[2],
            xprev(f[1], xb0[2, z]),
            yprev(f[2], side[2]),
        ]
        last = [
            (gz == 3) if z == 7 else None,
            (sx == 7) & (gx == 15),
            (ly == 127) & (gy == 7),
        ]
        first = [
            (gz == 0) if z == 0 else None,
            (sx == 0) & (gx == 0),
            (ly == 0) & (gy == 0),
        ]
        terms = []
        for d in range(3):
            up = 0.5 * (k[d] + kn[d]) + f[d] * (0.5 * (v[d] + vn[d]))
            down = 0.5 * (kp[d] + k[d]) + (1.0 - fp[d]) * (0.5 * (vp[d] + v[d]))
            if last[d] is not None:
                up = jnp.where(last[d], 0.0, up)
            if first[d] is not None:
                down = jnp.where(first[d], 0.0, down)
            terms += [up, down]
        rate = r_ref[z]
        diag = rate
        for term in terms:
            diag = diag + term
        scale = RELAX / diag
        d0[z] = diag * (1.0 / RELAX)
        for q in range(6):
            cu[q, z] = terms[q]
            scaled = terms[q] * scale
            ea[1 + q, 2 + z] = scaled
            start = 32 + 16 * q + 2 * z
            pack = jnp.where((ly >= start) & (ly < start + 2), roll(scaled, start + 1, 1), pack)
        begun = src_ref[z] * scale
        ea[0, 2 + z] = begun
        pack = jnp.where((ly >= 4 * z) & (ly < 4 * z + 4), roll(begun, 4 * z + 2, 1), pack)
    pk[...] = pack

    diagonal_y = [(0, 0, 1), (0, 0, -1)] + [(s, 0, t) for s in (1, -1) for t in (1, -1)] + [(0, s, t) for s in (1, -1) for t in (1, -1)]

    def rim(group, a, x, p, pr):
        for s in (1, -1):
            mine, theirs = (8, 0) if s == 1 else (2, 10)
            send(group, a.at[pl.ds(mine, 2)], a.at[pl.ds(theirs, 2)], (s, 0, 0))
            row = 6 if s == 1 else 0
            send(group, a.at[pl.ds(2, 8), pl.ds(row, 2)], x.at[pl.ds(1, 8), pl.ds(row, 2)], (0, s, 0))
        for i, offset in enumerate(diagonal_y):
            send(group, p, pr.at[i], offset)
        for s in (1, -1):
            for t in (1, -1):
                plane, row = (9 if s == 1 else 2), (7 if t == 1 else 0)
                there = x.at[pl.ds(0 if s == 1 else 9, 1), pl.ds(row, 1)]
                send(group, a.at[pl.ds(plane, 1), pl.ds(row, 1)], there, (s, t, 0))

    r1 = net.group()
    for s in (1, -1):
        mine, theirs, row = (9, 1, 7) if s == 1 else (2, 10, 0)
        send(r1, ea.at[pl.ds(1, 6), pl.ds(mine, 1)], ea.at[pl.ds(1, 6), pl.ds(theirs, 1)], (s, 0, 0))
        there = ex.at[pl.ds(1, 6), pl.ds(1, 8), pl.ds(row, 1)]
        send(r1, ea.at[pl.ds(1, 6), pl.ds(2, 8), pl.ds(row, 1)], there, (0, s, 0))
    rim(r1, ea.at[0], ex.at[0], pk, pkr)

    own1 = (iota((16, 128), 1) >= 32) & (iota((16, 128), 1) < 96)

    def scaled_terms(fields, inside):
        diag = fields[6]
        for q in range(6):
            diag = diag + fields[q]
        diag = jnp.where(inside, diag, 1.0)
        scale = jnp.where(inside, RELAX / diag, 0.0)
        return [fields[q] * scale for q in range(6)] + [jnp.where(inside, diag * (1.0 / RELAX), 0.0)]

    def pairs(q, a, b):
        pick = PICKS[q][0]
        return a + b if pick is None else (b if pick else a)

    def lanes01(pick):
        return mat(128, 128, lambda i, j: (j == 32 + (i >> 1)) & low_lanes(i, pick))

    def lanes12(pick):
        return mat(128, 128, lambda i, j: (j == 16 + (i >> 1)) & (i >= 32) & (i < 96) & low_lanes(i, pick))

    def lanes23(pick):
        return mat(128, 128, lambda i, j: (j == (i >> 1)) & (i >= 32) & (i < 64) & low_lanes(i, pick))

    def rows01(pick):
        return mat(16, 32, lambda i, j: ((j >> 3) == (i & 3)) & (((j & 7) >> 1) == (i >> 2)) & low_lanes(j, pick))

    def rows12(pz, px):
        return mat(
            8, 16,
            lambda i, j: ((j >> 3) == (i >> 1)) & (((j & 3) >> 1) == (i & 1)) & low_lanes(j, pz) & low_lanes(j >> 2, px),
        )

    def rows23(pz, px):
        return mat(8, 8, lambda i, j: (i == 0) & (j < 4) & low_lanes(j, pz) & low_lanes(j >> 1, px))

    def halves(block):
        return jnp.where(own8, block[0:8], roll(block[8:16], 64, 1))

    def zslot(k):
        return (4 - k) % 4

    def xplace(own, per, a):
        return own - per * a

    own8 = (ly >= 32) & (ly < 96)
    level1 = []
    for q in range(7):
        planes = [pairs(q, (cu[q, 2 * z] if q < 6 else r_ref[2 * z]), (cu[q, 2 * z + 1] if q < 6 else r_ref[2 * z + 1])) for z in range(4)]
        stacked = jnp.concatenate(planes, axis=0)
        level1.append(right(left(rows01(PICKS[q][1]), stacked), lanes01(PICKS[q][2])))
    scaled1 = scaled_terms(level1, own1)
    d1_own = scaled1[6]
    strip = jnp.zeros((8, 128), F32)
    for q in range(7):
        block = halves(scaled1[q])
        for x in range(2):
            p1[q, 1, x, 0:4, :] = block[4 * x : 4 * x + 4]
        if q < 6:
            for h in range(2):
                t = 4 * (2 * q + h)
                moved = roll(scaled1[q][8 * h : 8 * h + 8], t - 92, 1)
                strip = jnp.where(((ly >= t) & (ly < t + 4)) | ((ly >= t + 68) & (ly < t + 72)), moved, strip)
    for x in range(2):
        s1[x, 0:4, :] = strip[4 * x : 4 * x + 4]
    c1_copies = net.group()
    for k, a in ZX:
        n = 6 if a else 7
        there = p1.at[pl.ds(0, n), pl.ds(1 - a, 1), :, pl.ds(4 * zslot(k), 4)]
        send(c1_copies, p1.at[pl.ds(0, n), pl.ds(1, 1), :, pl.ds(0, 4)], there, (k, a, 0))
    pl.semaphore_wait(go_c, 2)
    for k, a in [(0, 0)] + ZX:
        for t in (1, -1):
            there = s1l if t == 1 else s1h
            send(c1_copies, s1.at[:, pl.ds(0, 4)], there.at[1 - a, :, pl.ds(4 * zslot(k), 4)], (k, a, t))

    level2 = [right(left(rows12(PICKS[q][0], PICKS[q][1]), level1[q]), lanes12(PICKS[q][2])) for q in range(7)]
    level3 = [right(left(rows23(PICKS[q][0], PICKS[q][1]), level2[q]), lanes23(PICKS[q][2])) for q in range(7)]
    inside2 = (ly >= 32) & (ly < 64) & (sx < 4)
    inside3 = (ly >= 16) & (ly < 32) & (sx < 1)
    scaled2 = scaled_terms(level2, inside2)
    scaled3 = scaled_terms(level3, inside3)
    group = [jnp.zeros((8, 128), F32), jnp.zeros((8, 128), F32)]
    line = jnp.zeros((8, 128), F32)
    for q in range(7):
        g, j = q // 4, q % 4
        group[g] = group[g] + roll(scaled2[q], 32 * j - 32, 1)
        line = line + roll(scaled3[q], 16 * q - 16, 1)
    for g in range(2):
        for x in range(2):
            a2[1, 2 * g + x, 0:2, :] = group[g][2 * x : 2 * x + 2]
    a3[1, 0:1, :] = line[0:1]
    z_copies = net.group()
    for k in range(4):
        for t in (0, 1, -1):
            if k or t:
                there = a2.at[pl.ds(1 - t, 1), :, pl.ds(2 * zslot(k), 2)]
                send(z_copies, a2.at[pl.ds(1, 1), :, pl.ds(0, 2)], there, (k, 0, t))
                send(z_copies, a3.at[pl.ds(1, 1), pl.ds(0, 1)], a3.at[pl.ds(1 - t, 1), pl.ds(zslot(k), 1)], (k, 0, t))

    wait(r1)
    pl.semaphore_wait(go_a, 2)
    for a in (4, -4):
        net.signal(go_b, (0, a, 0))

    def unpack(pr, y, xy):
        from_low = (ly & jnp.where(ly < 32, 2, 1)) == 0

        def both(low, high):
            return jnp.where(from_low, pr[low], pr[high])

        beside = both(0, 1)
        for z in range(8):
            y[1 + z] = roll(beside, -(4 * z + 2), 1)
        y[0] = roll(both(2, 3), -30, 1)
        y[9] = roll(both(4, 5), -2, 1)
        across = jnp.where(sx < 4, both(8, 9), both(6, 7))
        for z in range(8):
            xy[z] = roll(across, -(4 * z + 2), 1)
        return beside

    beside = unpack(pkr, ey.at[0], exy)
    for q in range(6):
        for z in range(8):
            ey[1 + q, 1 + z] = roll(beside, -(32 + 16 * q + 2 * z + 1), 1)

    def sweep(here, zp, zn, xp, xn, yp, yn, rhs, s):
        total = KEEP * here + rhs
        total = total + s[0] * zn + s[1] * zp
        total = total + s[2] * xn + s[3] * xp
        return total + s[4] * yn + s[5] * yp

    def sweep_a(a, x, y, p, outer):
        here = a[p]
        bx, by = x[p - outer], y[p - outer]
        return sweep(
            here, a[p - 1], a[p + 1], xprev(here, bx), xnext(here, bx), yprev(here, by), ynext(here, by),
            ea[0, p], [ea[1 + q, p] for q in range(6)],
        )

    def rim_sweep(a, x, y, xy):
        for p in range(1, 11):
            va[p] = sweep_a(a, x, y, p, 1)
        for z in range(8):
            here = x[1 + z]
            ba, bxy = a[2 + z], xy[z]
            vx[z] = sweep(
                here, x[z], x[2 + z], xprev(here, ba), xnext(here, ba), yprev(here, bxy), ynext(here, bxy),
                ex[0, 1 + z], [ex[1 + q, 1 + z] for q in range(6)],
            )
            here = y[1 + z]
            vy[z] = sweep(
                here, y[z], y[2 + z], xprev(here, bxy), xnext(here, bxy), yprev(here, ba), ynext(here, ba),
                ey[0, 1 + z], [ey[1 + q, 1 + z] for q in range(6)],
            )

    rim_sweep(ea.at[0], ex.at[0], ey.at[0], exy)
    planes = []
    for z in range(4):
        two = [(sweep_a(va, vx, vy, 2 + p, 2) - va[2 + p]) * d0[p] for p in (2 * z, 2 * z + 1)]
        planes.append(two[0] + two[1])
    rhs1 = right(left(rows01(None), jnp.concatenate(planes, axis=0)), lanes01(None))
    rhs1 = halves(jnp.where(own1, rhs1 / jnp.where(own1, d1_own, 1.0), 0.0))
    for x in range(2):
        b1c[1, 1, x, 0:4, :] = rhs1[4 * x : 4 * x + 4]

    r2 = net.group()
    for t in (0, 1, -1):
        for k, a in [(0, 0)] + ZX:
            if (k, a, t) != (0, 0, 0):
                there = b1c.at[1 - t, 1 - a, :, pl.ds(4 * zslot(k), 4)]
                send(r2, b1c.at[1, 1, :, pl.ds(0, 4)], there, (k, a, t))

    pack = jnp.zeros((8, 128), F32)
    for z in range(8):
        plane = va[2 + z]
        wa[2 + z] = plane
        pack = jnp.where((ly >= 4 * z) & (ly < 4 * z + 4), roll(plane, 4 * z + 2, 1), pack)
    wpk[...] = pack
    up0 = net.group()
    rim(up0, wa, wx, wpk, wpkr)

    wait(z_copies)
    for q in range(7):
        g, j = q // 4, q % 4
        for x in range(2):
            low, mid, high = [roll(a2[t, 2 * g + x], 32 * t - 32 * j, 1) for t in range(3)]
            c2[q, 6 + x] = jnp.where(ly < 32, low, jnp.where(ly < 64, mid, jnp.where(ly < 96, high, 0.0)))
    c2_copies = net.group()
    for a in (1, -1, 2, -2, 3, -3):
        send(c2_copies, c2.at[pl.ds(0, 6), pl.ds(6, 2)], c2.at[pl.ds(0, 6), pl.ds(xplace(6, 2, a), 2)], (0, a, 0))
    fields3 = []
    for q in range(7):
        low, mid, high = [roll(a3[t], 16 * t - 16 * q, 1) for t in range(3)]
        fields3.append(jnp.where(ly < 16, low, jnp.where(ly < 32, mid, jnp.where(ly < 48, high, 0.0))))
    for q in range(3):
        c3[q, 0] = jnp.where(ly < 64, fields3[2 * q], roll(fields3[2 * q + 1], 64, 1))

    def sweep_l(v, b, c, x):
        here = v[x]
        return sweep(
            here, roll(here, 1, 0), roll(here, -1, 0), v[x - 1], v[x + 1], roll(here, 1, 1), roll(here, -1, 1),
            b[x], [c[q, x] for q in range(6)],
        )

    wait(c1_copies)
    lane16 = iota((16, 128), 1)
    own16 = (lane16 >= 32) & (lane16 < 96)
    for i in range(3):
        for x in range(2):
            rims = jnp.where(lane16 < 64, s1l[i, x], s1h[i, x])
            for q in range(6):
                block = p1[q, i, x]
                c1[q, 4 * i + x] = jnp.where(own16, block, roll(rims, 28 - 8 * q, 1))
                c1[q, 4 * i + 2 + x] = jnp.where(own16, roll(block, 64, 1), roll(rims, 24 - 8 * q, 1))
    for x in range(2):
        block = p1[6, 1, x]
        c1[6, 4 + x] = block
        c1[6, 6 + x] = roll(block, 64, 1)
    wait(r2)
    for i in range(3):
        for x in range(2):
            low, mid, high = [b1c[t, i, x] for t in range(3)]
            b1[4 * i + x] = jnp.where(own16, mid, roll(jnp.where(lane16 >= 64, low, high), 64, 1))
            b1[4 * i + 2 + x] = jnp.where(own16, roll(mid, 64, 1), jnp.where(lane16 < 64, low, high))
    for x in range(1, 11):
        v1p[x] = sweep_l(b1, b1, c1, x)
    rows = []
    for x in range(2):
        two = [(sweep_l(v1p, b1, c1, p) - v1p[p]) * c1[6, p] for p in (4 + 2 * x, 5 + 2 * x)]
        rows.append(two[0] + two[1])
    rows = right(jnp.concatenate(rows, axis=0), lanes12(None))
    halve = mat(8, 16, lambda i, j: (j >> 1) == i)
    for x in range(2):
        inside = (ly >= 32) & (ly < 64)
        rhs2 = left(halve, rows[16 * x : 16 * x + 16])
        rhs2 = jnp.where(inside, rhs2 / jnp.where(inside, c2[6, 6 + x], 1.0), 0.0)
        b2c[6 + x] = rhs2
        b2r[x] = roll(rhs2, 32, 1) + roll(rhs2, -32, 1)

    r3 = net.group()
    for a in (0, 1, -1, 2, -2, 3, -3):
        there = pl.ds(xplace(6, 2, a), 2)
        if a:
            send(r3, b2c.at[pl.ds(6, 2)], b2c.at[there], (0, a, 0))
        send(r3, b2r, b2l.at[there], (0, a, 1))
        send(r3, b2r, b2h.at[there], (0, a, -1))
    pl.semaphore_wait(go_b, 2)
    c3_copies = net.group()
    for a in range(1, 16):
        send(c3_copies, c3.at[:, pl.ds(0, 1), pl.ds(0, 4)], c3.at[:, pl.ds(16 - a, 1), pl.ds(0, 4)], (0, a, 0))

    wait(c2_copies)
    wait(r3)
    for x in range(14):
        b2[x] = jnp.where(ly < 32, b2l[x], jnp.where(ly >= 64, b2h[x], b2c[x]))
    for x in range(2, 12):
        v2p[x] = sweep_l(b2, b2, c2, x)
    two = [(sweep_l(v2p, b2, c2, p) - v2p[p]) * c2[6, p] for p in (6, 7)]
    rows = right(two[0] + two[1], mat(128, 128, lambda i, j: (j == (i >> 1)) & (i < 96)))
    rhs3 = left(mat(8, 8, lambda i, j: (j >> 1) == (i & 3)), rows)

    def twice(block):
        return jnp.where(sx < 4, block, roll(block, 4, 0))

    inside = ly < 48
    rhs3 = jnp.where(inside, rhs3 / jnp.where(inside, twice(fields3[6]), 1.0), 0.0)
    b3[0] = rhs3

    r4 = net.group()
    for a in range(1, 16):
        send(r4, b3.at[pl.ds(0, 1)], b3.at[pl.ds(16 - a, 1)], (0, a, 0))
    wait(c3_copies)
    terms3 = []
    for q in range(3):
        terms3.append([twice(c3[q, x]) for x in range(16)])
        terms3.append([roll(block, 64, 1) for block in terms3[-1]])
    wait(r4)
    rhs3 = [b3[x] for x in range(16)]
    here = rhs3
    for _ in range(7):
        here = [
            sweep(
                here[x], roll(here[x], 1, 0), roll(here[x], -1, 0), here[(x + 15) % 16], here[(x + 1) % 16],
                roll(here[x], 1, 1), roll(here[x], -1, 1), rhs3[x], [terms3[q][x] for q in range(6)],
            )
            for x in range(16)
        ]

    wide = left(mat(8, 8, lambda i, j: j == (i >> 1)), jnp.concatenate([here[(X + 16) % 16] for X in range(-2, 3)], axis=1))
    wide = jnp.concatenate([wide[:, 128 * i : 128 * i + 128] for i in range(5)], axis=0)
    wide = right(wide, mat(128, 128, lambda i, j: (i == (j >> 1)) & (j < 96)))
    for x in range(2, 12):
        i = (x >> 1) - 1
        v2p[x] = v2p[x] + wide[8 * i : 8 * i + 8]
    for x in range(3, 11):
        v2q[x] = sweep_l(v2p, b2, c2, x)
    ups = [sweep_l(v2q, b2, c2, x) for x in range(4, 10)]

    wide = right(jnp.concatenate(ups, axis=0), mat(128, 128, lambda i, j: i == 16 + (j >> 1)))
    wide = left(mat(16, 8, lambda i, j: j == (i >> 1)), jnp.concatenate([wide[8 * i : 8 * i + 8] for i in range(6)], axis=1))
    for x in range(1, 11):
        i = x >> 1
        v1p[x] = v1p[x] + wide[:, 128 * i : 128 * i + 128]
    for x in range(2, 10):
        v1q[x] = sweep_l(v1p, b1, c1, x)
    ups = [sweep_l(v1q, b1, c1, x) for x in range(3, 9)]

    def lanes10(i, j):
        main = (j < 128) & (i == 32 + (j >> 1))
        return main | ((j >= 254) & (i == 31)) | ((j >= 128) & (j < 130) & (i == 96))

    def rows10(i, j):
        xi, zr = j >> 4, j & 15
        main = (i < 96) & (zr == (((i >> 4) + 15) & 15)) & (xi == 1 + ((i & 7) >> 1))
        n = i - 96
        beside = (i >= 96) & (zr == ((((n >> 3) + 31) >> 1) & 15)) & (
            (((n & 7) >= 6) & (xi == 0)) | (((n & 7) < 2) & (xi == 5))
        )
        return main | beside

    wide = right(jnp.concatenate(ups, axis=0), mat(128, 256, lanes10))
    wide = left(mat(176, 96, rows10), wide)
    wait(up0)
    low = (ly & 2) == 0
    beside = jnp.where(low, wpkr[0], wpkr[1])
    low_z = jnp.where(low, wpkr[2], wpkr[3])
    high_z = jnp.where(low, wpkr[4], wpkr[5])
    across = jnp.where(sx < 4, jnp.where(low, wpkr[8], wpkr[9]), jnp.where(low, wpkr[6], wpkr[7]))
    a = [wa[p] + wide[8 * p : 8 * p + 8, 0:128] for p in range(12)]
    x = [wx[p] + wide[96 + 8 * p : 104 + 8 * p, 0:128] for p in range(10)]
    y = []
    for p in range(10):
        if p == 0:
            base = roll(low_z, -30, 1)
        elif p == 9:
            base = roll(high_z, -2, 1)
        else:
            base = roll(beside, -(4 * (p - 1) + 2), 1)
        y.append(base + wide[8 * (p + 1) : 8 * (p + 1) + 8, 128:256])
    xy = [roll(across, -(4 * z + 2), 1) + wide[104 + 8 * z : 112 + 8 * z, 128:256] for z in range(8)]
    rim_sweep(a, x, y, xy)
    for z in range(8):
        out_ref[z] = sweep_a(va, vx, vy, 2 + z, 2)
    net.finish()


def on_device(source, decay_rate, dispersion, velocity, upwind):
    def vmem(*shape):
        return pltpu.VMEM(shape, F32)

    tile = (8, 128)
    scratch = [
        vmem(8, *tile), vmem(8, *tile), vmem(3, 8, *tile), vmem(3, 8, *tile), pltpu.VMEM((3, 8, *tile), jnp.int32),
        pltpu.SemaphoreType.DMA((5,)),
        vmem(3, 8, *tile), vmem(5, *tile), vmem(*tile), vmem(3, 8, *tile), vmem(3, *tile), vmem(2, *tile), vmem(*tile), vmem(*tile),
        vmem(7, 12, *tile), vmem(7, 10, *tile), vmem(7, 10, *tile), vmem(8, *tile), vmem(*tile), vmem(10, *tile),
        vmem(6, 8, *tile), vmem(8, *tile), vmem(12, *tile), vmem(8, *tile), vmem(8, *tile),
        vmem(12, *tile), vmem(10, *tile), vmem(*tile), vmem(10, *tile),
        vmem(7, 3, 2, 16, 128), vmem(2, *tile), vmem(3, 2, 16, 128), vmem(3, 2, 16, 128), vmem(3, 4, *tile), vmem(3, *tile),
        vmem(7, 12, 16, 128), vmem(7, 14, *tile), vmem(3, 16, *tile),
        vmem(3, 3, 2, 16, 128), vmem(12, 16, 128), vmem(12, 16, 128), vmem(12, 16, 128),
        vmem(14, *tile), vmem(2, *tile), vmem(14, *tile), vmem(14, *tile), vmem(14, *tile), vmem(14, *tile), vmem(14, *tile),
        vmem(16, *tile),
        pltpu.SemaphoreType.REGULAR, pltpu.SemaphoreType.REGULAR, pltpu.SemaphoreType.REGULAR,
        vmem(768, 128), pltpu.SemaphoreType.DMA((GROUPS,)), pltpu.SemaphoreType.DMA((GROUPS,)),
    ]
    return pl.pallas_call(
        kernel,
        out_shape=jax.ShapeDtypeStruct((8, 8, 128), F32),
        in_specs=[pl.BlockSpec(memory_space=pltpu.HBM)] * 5,
        out_specs=pl.BlockSpec(memory_space=pltpu.VMEM),
        scratch_shapes=scratch,
        compiler_params=pltpu.CompilerParams(
            collective_id=0, has_side_effects=True, vmem_limit_bytes=32 * 1024 * 1024
        ),
    )(source, decay_rate, dispersion, velocity, upwind)


def solution(mesh):
    field, vector = P("gz", "gx", "gy"), P(None, "gz", "gx", "gy")
    return jax.shard_map(
        on_device, mesh=mesh, in_specs=(field, field, vector, vector, vector), out_specs=field, check_vma=False
    )
```

```python
import jax
import jax.numpy as jnp
from jax import lax
from jax.experimental import pallas as pl
from jax.experimental.pallas import tpu as pltpu
from jax.sharding import PartitionSpec as P

MESH = pl.DeviceIdType.MESH
SIZES = (("gz", 4), ("gx", 16), ("gy", 8))
F32 = jnp.float32
RELAX = 0.7
KEEP = 1.0 - RELAX
GROUPS = 10

ZX = [(k, a) for k in range(4) for a in (0, 1, -1) if (k, a) != (0, 0)]


class Net:
    def __init__(self, tally, send_sems, recv_sems):
        self.tally, self.send_sems, self.recv_sems = tally, send_sems, recv_sems
        self.rows, self.places = [], {}
        for name, size in SIZES:
            here = lax.axis_index(name)
            for step in range(size):
                self.places[name, step] = (here + step) & (size - 1) if step else here

    def at(self, offset):
        return {name: self.places[name, step % size] for (name, size), step in zip(SIZES, offset)}

    def signal(self, sem, offset):
        pl.semaphore_signal(sem, inc=1, device_id=self.at(offset), device_id_type=MESH)

    def group(self):
        self.rows.append(0)
        return len(self.rows) - 1

    def send(self, group, src, dst, offset):
        size = 1
        for n in src.shape:
            size *= n
        self.rows[group] += size // 128
        pltpu.make_async_remote_copy(
            src_ref=src,
            dst_ref=dst,
            send_sem=self.send_sems.at[group],
            recv_sem=self.recv_sems.at[group],
            device_id=self.at(offset),
            device_id_type=MESH,
        ).start()

    def whole(self, group):
        part = self.tally.at[pl.ds(0, self.rows[group])]
        return pltpu.make_async_remote_copy(
            src_ref=part,
            dst_ref=part,
            send_sem=self.send_sems.at[group],
            recv_sem=self.recv_sems.at[group],
            device_id=self.at((0, 0, 1)),
            device_id_type=MESH,
        )

    def wait(self, group):
        self.whole(group).wait_recv()

    def finish(self):
        for group in range(len(self.rows)):
            self.whole(group).wait_send()


def iota(shape, dim):
    return lax.broadcasted_iota(jnp.int32, shape, dim)


def mat(rows, cols, where):
    return jnp.where(where(iota((rows, cols), 0), iota((rows, cols), 1)), 1.0, 0.0).astype(F32)


def split(x):
    high = x.astype(jnp.bfloat16)
    return high, (x - high.astype(F32)).astype(jnp.bfloat16)


def dot(a, b, ones):
    if ones:
        b = b.astype(jnp.bfloat16)
        pairs = [(part, b) for part in split(a)]
    else:
        a = a.astype(jnp.bfloat16)
        pairs = [(a, part) for part in split(b)]
    high, low = [jnp.dot(x, y, preferred_element_type=F32) for x, y in pairs]
    return high + low


def left(a, b):
    return dot(a, b, 0)


def right(a, b):
    return dot(a, b, 1)


def roll(x, shift, axis):
    size = x.shape[axis]
    shift = shift % size
    return pltpu.roll(x, shift, axis) if shift else x


def low_lanes(i, parity):
    if parity is None:
        return i >= 0
    return (i & 1) == parity


PICKS = ((1, None, None), (0, None, None), (None, 1, None), (None, 0, None), (None, None, 1), (None, None, 0), (None, None, None))


def kernel(
    src_hbm, r_hbm, k_hbm, v_hbm, f_hbm, out_ref,
    src_ref, r_ref, k_ref, v_ref, f_ref, in_sems,
    e0a, e0z, e0y, xb0, zlo, zhi, ylo, yhi,
    ea, ex, ey, exy, pk, pkr,
    cu, d0, va, vx, vy,
    wa, wx, wpk, wpkr,
    p1, s1, s1l, s1h, a2, a3, c1, c2, c3,
    b1c, b1, v1p, v1q,
    b2c, b2r, b2l, b2h, b2, v2p, v2q,
    b3, go_a, go_b, go_c, tally, ssem, rsem,
):
    net = Net(tally, ssem, rsem)
    send, wait = net.send, net.wait
    gz, gx, gy = lax.axis_index("gz"), lax.axis_index("gx"), lax.axis_index("gy")
    sx, ly = iota((8, 128), 0), iota((8, 128), 1)

    fetches = [
        pltpu.make_async_copy(here, there, in_sems.at[i])
        for i, (here, there) in enumerate(
            ((k_hbm, k_ref), (v_hbm, v_ref), (f_hbm, f_ref), (src_hbm, src_ref), (r_hbm, r_ref))
        )
    ]
    for fetch in fetches:
        fetch.start()
    barrier = pltpu.get_barrier_semaphore()
    greeted = [(1, 0, 0), (2, 0, 0), (3, 0, 0), (0, 1, 0), (0, -1, 0), (0, 0, 1), (0, 0, -1)]
    for offset in greeted:
        net.signal(barrier, offset)

    for fetch in fetches[:3]:
        fetch.wait()
    e0a[0] = k_ref[1]
    e0a[1] = v_ref[1]
    e0a[2] = f_ref[1].astype(F32)
    e0z[0] = k_ref[0, 7]
    e0z[1] = v_ref[0, 7]
    e0z[2] = f_ref[0, 7].astype(F32)
    e0z[3] = k_ref[0, 0]
    e0z[4] = v_ref[0, 0]
    packed = jnp.zeros((8, 128), F32)
    for f, ref in enumerate((k_ref, v_ref, f_ref)):
        for z in range(8):
            start = 16 * f + 2 * z
            moved = roll(ref[2, z].astype(F32), start + 1, 1)
            packed = jnp.where((ly >= start) & (ly < start + 2), moved, packed)
    e0y[...] = packed
    pl.semaphore_wait(barrier, len(greeted))
    e0 = net.group()
    send(e0, e0a.at[:, :, pl.ds(7, 1), :], xb0.at[:, :, pl.ds(7, 1), :], (0, 1, 0))
    send(e0, e0a.at[pl.ds(0, 2), :, pl.ds(0, 1), :], xb0.at[pl.ds(0, 2), :, pl.ds(0, 1), :], (0, -1, 0))
    send(e0, e0z.at[pl.ds(0, 3)], zlo, (1, 0, 0))
    send(e0, e0z.at[pl.ds(3, 2)], zhi, (-1, 0, 0))
    send(e0, e0y, ylo, (0, 0, 1))
    send(e0, e0y, yhi, (0, 0, -1))

    def xprev(a, b):
        return roll(jnp.where(sx == 7, b, a), 1, 0)

    def xnext(a, b):
        return roll(jnp.where(sx == 0, b, a), -1, 0)

    def yprev(a, b):
        return roll(jnp.where(ly == 127, b, a), 1, 1)

    def ynext(a, b):
        return roll(jnp.where(ly == 0, b, a), -1, 1)

    wait(e0)
    for a in (2, -2):
        net.signal(go_a, (0, a, 0))
    for t in (1, -1):
        net.signal(go_c, (0, 0, t))
    for fetch in fetches[3:]:
        fetch.wait()

    both0 = jnp.where((ly & 1) == 0, ylo[...], yhi[...])
    pack = jnp.zeros((8, 128), F32)
    for z in range(8):
        k, v = [k_ref[d, z] for d in range(3)], [v_ref[d, z] for d in range(3)]
        f = [f_ref[d, z].astype(F32) for d in range(3)]
        side = [roll(both0, -(16 * q + 2 * z + 1), 1) for q in range(3)]
        kn = [
            k_ref[0, z + 1] if z < 7 else zhi[0],
            xnext(k[1], xb0[0, z]),
            ynext(k[2], side[0]),
        ]
        vn = [
            v_ref[0, z + 1] if z < 7 else zhi[1],
            xnext(v[1], xb0[1, z]),
            ynext(v[2], side[1]),
        ]
        kp = [
            k_ref[0, z - 1] if z else zlo[0],
            xprev(k[1], xb0[0, z]),
            yprev(k[2], side[0]),
        ]
        vp = [
            v_ref[0, z - 1] if z else zlo[1],
            xprev(v[1], xb0[1, z]),
            yprev(v[2], side[1]),
        ]
        fp = [
            f_ref[0, z - 1].astype(F32) if z else zlo[2],
            xprev(f[1], xb0[2, z]),
            yprev(f[2], side[2]),
        ]
        last = [
            (gz == 3) if z == 7 else None,
            (sx == 7) & (gx == 15),
            (ly == 127) & (gy == 7),
        ]
        first = [
            (gz == 0) if z == 0 else None,
            (sx == 0) & (gx == 0),
            (ly == 0) & (gy == 0),
        ]
        terms = []
        for d in range(3):
            up = 0.5 * (k[d] + kn[d]) + f[d] * (0.5 * (v[d] + vn[d]))
            down = 0.5 * (kp[d] + k[d]) + (1.0 - fp[d]) * (0.5 * (vp[d] + v[d]))
            if last[d] is not None:
                up = jnp.where(last[d], 0.0, up)
            if first[d] is not None:
                down = jnp.where(first[d], 0.0, down)
            terms += [up, down]
        rate = r_ref[z]
        diag = rate
        for term in terms:
            diag = diag + term
        scale = RELAX / diag
        d0[z] = diag * (1.0 / RELAX)
        for q in range(6):
            cu[q, z] = terms[q]
            scaled = terms[q] * scale
            ea[1 + q, 2 + z] = scaled
            start = 32 + 16 * q + 2 * z
            pack = jnp.where((ly >= start) & (ly < start + 2), roll(scaled, start + 1, 1), pack)
        begun = src_ref[z] * scale
        ea[0, 2 + z] = begun
        pack = jnp.where((ly >= 4 * z) & (ly < 4 * z + 4), roll(begun, 4 * z + 2, 1), pack)
    pk[...] = pack

    diagonal_y = [(0, 0, 1), (0, 0, -1)] + [(s, 0, t) for s in (1, -1) for t in (1, -1)] + [(0, s, t) for s in (1, -1) for t in (1, -1)]

    def rim(group, a, x, p, pr):
        for s in (1, -1):
            mine, theirs = (8, 0) if s == 1 else (2, 10)
            send(group, a.at[pl.ds(mine, 2)], a.at[pl.ds(theirs, 2)], (s, 0, 0))
            row = 6 if s == 1 else 0
            send(group, a.at[pl.ds(2, 8), pl.ds(row, 2)], x.at[pl.ds(1, 8), pl.ds(row, 2)], (0, s, 0))
        for i, offset in enumerate(diagonal_y):
            send(group, p, pr.at[i], offset)
        for s in (1, -1):
            for t in (1, -1):
                plane, row = (9 if s == 1 else 2), (7 if t == 1 else 0)
                there = x.at[pl.ds(0 if s == 1 else 9, 1), pl.ds(row, 1)]
                send(group, a.at[pl.ds(plane, 1), pl.ds(row, 1)], there, (s, t, 0))

    r1 = net.group()
    for s in (1, -1):
        mine, theirs, row = (9, 1, 7) if s == 1 else (2, 10, 0)
        send(r1, ea.at[pl.ds(1, 6), pl.ds(mine, 1)], ea.at[pl.ds(1, 6), pl.ds(theirs, 1)], (s, 0, 0))
        there = ex.at[pl.ds(1, 6), pl.ds(1, 8), pl.ds(row, 1)]
        send(r1, ea.at[pl.ds(1, 6), pl.ds(2, 8), pl.ds(row, 1)], there, (0, s, 0))
    rim(r1, ea.at[0], ex.at[0], pk, pkr)

    own1 = (iota((16, 128), 1) >= 32) & (iota((16, 128), 1) < 96)

    def scaled_terms(fields, inside):
        diag = fields[6]
        for q in range(6):
            diag = diag + fields[q]
        diag = jnp.where(inside, diag, 1.0)
        scale = jnp.where(inside, RELAX / diag, 0.0)
        return [fields[q] * scale for q in range(6)] + [jnp.where(inside, diag * (1.0 / RELAX), 0.0)]

    def pairs(q, a, b):
        pick = PICKS[q][0]
        return a + b if pick is None else (b if pick else a)

    def lanes01(pick):
        return mat(128, 128, lambda i, j: (j == 32 + (i >> 1)) & low_lanes(i, pick))

    def lanes12(pick):
        return mat(128, 128, lambda i, j: (j == 16 + (i >> 1)) & (i >= 32) & (i < 96) & low_lanes(i, pick))

    def lanes23(pick):
        return mat(128, 128, lambda i, j: (j == (i >> 1)) & (i >= 32) & (i < 64) & low_lanes(i, pick))

    def rows01(pick):
        return mat(16, 32, lambda i, j: ((j >> 3) == (i & 3)) & (((j & 7) >> 1) == (i >> 2)) & low_lanes(j, pick))

    def rows12(pz, px):
        return mat(
            8, 16,
            lambda i, j: ((j >> 3) == (i >> 1)) & (((j & 3) >> 1) == (i & 1)) & low_lanes(j, pz) & low_lanes(j >> 2, px),
        )

    def rows23(pz, px):
        return mat(8, 8, lambda i, j: (i == 0) & (j < 4) & low_lanes(j, pz) & low_lanes(j >> 1, px))

    def halves(block):
        return jnp.where(own8, block[0:8], roll(block[8:16], 64, 1))

    def zslot(k):
        return (4 - k) % 4

    def xplace(own, per, a):
        return own - per * a

    own8 = (ly >= 32) & (ly < 96)
    level1 = []
    for q in range(7):
        planes = [pairs(q, (cu[q, 2 * z] if q < 6 else r_ref[2 * z]), (cu[q, 2 * z + 1] if q < 6 else r_ref[2 * z + 1])) for z in range(4)]
        stacked = jnp.concatenate(planes, axis=0)
        level1.append(right(left(rows01(PICKS[q][1]), stacked), lanes01(PICKS[q][2])))
    scaled1 = scaled_terms(level1, own1)
    d1_own = scaled1[6]
    strip = jnp.zeros((8, 128), F32)
    for q in range(7):
        block = halves(scaled1[q])
        for x in range(2):
            p1[q, 1, x, 0:4, :] = block[4 * x : 4 * x + 4]
        if q < 6:
            for h in range(2):
                t = 4 * (2 * q + h)
                moved = roll(scaled1[q][8 * h : 8 * h + 8], t - 92, 1)
                strip = jnp.where(((ly >= t) & (ly < t + 4)) | ((ly >= t + 68) & (ly < t + 72)), moved, strip)
    for x in range(2):
        s1[x, 0:4, :] = strip[4 * x : 4 * x + 4]
    c1_copies = net.group()
    for k, a in ZX:
        n = 6 if a else 7
        there = p1.at[pl.ds(0, n), pl.ds(1 - a, 1), :, pl.ds(4 * zslot(k), 4)]
        send(c1_copies, p1.at[pl.ds(0, n), pl.ds(1, 1), :, pl.ds(0, 4)], there, (k, a, 0))
    pl.semaphore_wait(go_c, 2)
    for k, a in [(0, 0)] + ZX:
        for t in (1, -1):
            there = s1l if t == 1 else s1h
            send(c1_copies, s1.at[:, pl.ds(0, 4)], there.at[1 - a, :, pl.ds(4 * zslot(k), 4)], (k, a, t))

    level2 = [right(left(rows12(PICKS[q][0], PICKS[q][1]), level1[q]), lanes12(PICKS[q][2])) for q in range(7)]
    level3 = [right(left(rows23(PICKS[q][0], PICKS[q][1]), level2[q]), lanes23(PICKS[q][2])) for q in range(7)]
    inside2 = (ly >= 32) & (ly < 64) & (sx < 4)
    inside3 = (ly >= 16) & (ly < 32) & (sx < 1)
    scaled2 = scaled_terms(level2, inside2)
    scaled3 = scaled_terms(level3, inside3)
    group = [jnp.zeros((8, 128), F32), jnp.zeros((8, 128), F32)]
    line = jnp.zeros((8, 128), F32)
    for q in range(7):
        g, j = q // 4, q % 4
        group[g] = group[g] + roll(scaled2[q], 32 * j - 32, 1)
        line = line + roll(scaled3[q], 16 * q - 16, 1)
    for g in range(2):
        for x in range(2):
            a2[1, 2 * g + x, 0:2, :] = group[g][2 * x : 2 * x + 2]
    a3[1, 0:1, :] = line[0:1]
    z_copies = net.group()
    for k in range(4):
        for t in (0, 1, -1):
            if k or t:
                there = a2.at[pl.ds(1 - t, 1), :, pl.ds(2 * zslot(k), 2)]
                send(z_copies, a2.at[pl.ds(1, 1), :, pl.ds(0, 2)], there, (k, 0, t))
                send(z_copies, a3.at[pl.ds(1, 1), pl.ds(0, 1)], a3.at[pl.ds(1 - t, 1), pl.ds(zslot(k), 1)], (k, 0, t))

    wait(r1)
    pl.semaphore_wait(go_a, 2)
    for a in (4, -4):
        net.signal(go_b, (0, a, 0))

    def unpack(pr, y, xy):
        from_low = (ly & jnp.where(ly < 32, 2, 1)) == 0

        def both(low, high):
            return jnp.where(from_low, pr[low], pr[high])

        beside = both(0, 1)
        for z in range(8):
            y[1 + z] = roll(beside, -(4 * z + 2), 1)
        y[0] = roll(both(2, 3), -30, 1)
        y[9] = roll(both(4, 5), -2, 1)
        across = jnp.where(sx < 4, both(8, 9), both(6, 7))
        for z in range(8):
            xy[z] = roll(across, -(4 * z + 2), 1)
        return beside

    beside = unpack(pkr, ey.at[0], exy)
    for q in range(6):
        for z in range(8):
            ey[1 + q, 1 + z] = roll(beside, -(32 + 16 * q + 2 * z + 1), 1)

    def sweep(here, zp, zn, xp, xn, yp, yn, rhs, s):
        total = KEEP * here + rhs
        total = total + s[0] * zn + s[1] * zp
        total = total + s[2] * xn + s[3] * xp
        return total + s[4] * yn + s[5] * yp

    def sweep_a(a, x, y, p, outer):
        here = a[p]
        bx, by = x[p - outer], y[p - outer]
        return sweep(
            here, a[p - 1], a[p + 1], xprev(here, bx), xnext(here, bx), yprev(here, by), ynext(here, by),
            ea[0, p], [ea[1 + q, p] for q in range(6)],
        )

    def rim_sweep(a, x, y, xy):
        for p in range(1, 11):
            va[p] = sweep_a(a, x, y, p, 1)
        for z in range(8):
            here = x[1 + z]
            ba, bxy = a[2 + z], xy[z]
            vx[z] = sweep(
                here, x[z], x[2 + z], xprev(here, ba), xnext(here, ba), yprev(here, bxy), ynext(here, bxy),
                ex[0, 1 + z], [ex[1 + q, 1 + z] for q in range(6)],
            )
            here = y[1 + z]
            vy[z] = sweep(
                here, y[z], y[2 + z], xprev(here, bxy), xnext(here, bxy), yprev(here, ba), ynext(here, ba),
                ey[0, 1 + z], [ey[1 + q, 1 + z] for q in range(6)],
            )

    rim_sweep(ea.at[0], ex.at[0], ey.at[0], exy)
    planes = []
    for z in range(4):
        two = [(sweep_a(va, vx, vy, 2 + p, 2) - va[2 + p]) * d0[p] for p in (2 * z, 2 * z + 1)]
        planes.append(two[0] + two[1])
    rhs1 = right(left(rows01(None), jnp.concatenate(planes, axis=0)), lanes01(None))
    rhs1 = halves(jnp.where(own1, rhs1 / jnp.where(own1, d1_own, 1.0), 0.0))
    for x in range(2):
        b1c[1, 1, x, 0:4, :] = rhs1[4 * x : 4 * x + 4]

    r2 = net.group()
    for t in (0, 1, -1):
        for k, a in [(0, 0)] + ZX:
            if (k, a, t) != (0, 0, 0):
                there = b1c.at[1 - t, 1 - a, :, pl.ds(4 * zslot(k), 4)]
                send(r2, b1c.at[1, 1, :, pl.ds(0, 4)], there, (k, a, t))

    pack = jnp.zeros((8, 128), F32)
    for z in range(8):
        plane = va[2 + z]
        wa[2 + z] = plane
        pack = jnp.where((ly >= 4 * z) & (ly < 4 * z + 4), roll(plane, 4 * z + 2, 1), pack)
    wpk[...] = pack
    up0 = net.group()
    rim(up0, wa, wx, wpk, wpkr)

    wait(z_copies)
    for q in range(7):
        g, j = q // 4, q % 4
        for x in range(2):
            low, mid, high = [roll(a2[t, 2 * g + x], 32 * t - 32 * j, 1) for t in range(3)]
            c2[q, 6 + x] = jnp.where(ly < 32, low, jnp.where(ly < 64, mid, jnp.where(ly < 96, high, 0.0)))
    c2_copies = net.group()
    for a in (1, -1, 2, -2, 3, -3):
        send(c2_copies, c2.at[pl.ds(0, 6), pl.ds(6, 2)], c2.at[pl.ds(0, 6), pl.ds(xplace(6, 2, a), 2)], (0, a, 0))
    fields3 = []
    for q in range(7):
        low, mid, high = [roll(a3[t], 16 * t - 16 * q, 1) for t in range(3)]
        fields3.append(jnp.where(ly < 16, low, jnp.where(ly < 32, mid, jnp.where(ly < 48, high, 0.0))))
    for q in range(3):
        c3[q, 0] = jnp.where(ly < 64, fields3[2 * q], roll(fields3[2 * q + 1], 64, 1))

    def sweep_l(v, b, c, x):
        here = v[x]
        return sweep(
            here, roll(here, 1, 0), roll(here, -1, 0), v[x - 1], v[x + 1], roll(here, 1, 1), roll(here, -1, 1),
            b[x], [c[q, x] for q in range(6)],
        )

    wait(c1_copies)
    lane16 = iota((16, 128), 1)
    own16 = (lane16 >= 32) & (lane16 < 96)
    for i in range(3):
        for x in range(2):
            rims = jnp.where(lane16 < 64, s1l[i, x], s1h[i, x])
            for q in range(6):
                block = p1[q, i, x]
                c1[q, 4 * i + x] = jnp.where(own16, block, roll(rims, 28 - 8 * q, 1))
                c1[q, 4 * i + 2 + x] = jnp.where(own16, roll(block, 64, 1), roll(rims, 24 - 8 * q, 1))
    for x in range(2):
        block = p1[6, 1, x]
        c1[6, 4 + x] = block
        c1[6, 6 + x] = roll(block, 64, 1)
    wait(r2)
    for i in range(3):
        for x in range(2):
            low, mid, high = [b1c[t, i, x] for t in range(3)]
            b1[4 * i + x] = jnp.where(own16, mid, roll(jnp.where(lane16 >= 64, low, high), 64, 1))
            b1[4 * i + 2 + x] = jnp.where(own16, roll(mid, 64, 1), jnp.where(lane16 < 64, low, high))
    for x in range(1, 11):
        v1p[x] = sweep_l(b1, b1, c1, x)
    rows = []
    for x in range(2):
        two = [(sweep_l(v1p, b1, c1, p) - v1p[p]) * c1[6, p] for p in (4 + 2 * x, 5 + 2 * x)]
        rows.append(two[0] + two[1])
    rows = right(jnp.concatenate(rows, axis=0), lanes12(None))
    halve = mat(8, 16, lambda i, j: (j >> 1) == i)
    for x in range(2):
        inside = (ly >= 32) & (ly < 64)
        rhs2 = left(halve, rows[16 * x : 16 * x + 16])
        rhs2 = jnp.where(inside, rhs2 / jnp.where(inside, c2[6, 6 + x], 1.0), 0.0)
        b2c[6 + x] = rhs2
        b2r[x] = roll(rhs2, 32, 1) + roll(rhs2, -32, 1)

    r3 = net.group()
    for a in (0, 1, -1, 2, -2, 3, -3):
        there = pl.ds(xplace(6, 2, a), 2)
        if a:
            send(r3, b2c.at[pl.ds(6, 2)], b2c.at[there], (0, a, 0))
        send(r3, b2r, b2l.at[there], (0, a, 1))
        send(r3, b2r, b2h.at[there], (0, a, -1))
    pl.semaphore_wait(go_b, 2)
    c3_copies = net.group()
    for a in range(1, 16):
        send(c3_copies, c3.at[:, pl.ds(0, 1), pl.ds(0, 4)], c3.at[:, pl.ds(16 - a, 1), pl.ds(0, 4)], (0, a, 0))

    wait(c2_copies)
    wait(r3)
    for x in range(14):
        b2[x] = jnp.where(ly < 32, b2l[x], jnp.where(ly >= 64, b2h[x], b2c[x]))
    for x in range(2, 12):
        v2p[x] = sweep_l(b2, b2, c2, x)
    two = [(sweep_l(v2p, b2, c2, p) - v2p[p]) * c2[6, p] for p in (6, 7)]
    rows = right(two[0] + two[1], mat(128, 128, lambda i, j: (j == (i >> 1)) & (i < 96)))
    rhs3 = left(mat(8, 8, lambda i, j: (j >> 1) == (i & 3)), rows)

    def twice(block):
        return jnp.where(sx < 4, block, roll(block, 4, 0))

    inside = ly < 48
    rhs3 = jnp.where(inside, rhs3 / jnp.where(inside, twice(fields3[6]), 1.0), 0.0)
    b3[0] = rhs3

    r4 = net.group()
    for a in range(1, 16):
        send(r4, b3.at[pl.ds(0, 1)], b3.at[pl.ds(16 - a, 1)], (0, a, 0))
    wait(c3_copies)
    terms3 = []
    for q in range(3):
        terms3.append([twice(c3[q, x]) for x in range(16)])
        terms3.append([roll(block, 64, 1) for block in terms3[-1]])
    wait(r4)
    rhs3 = [b3[x] for x in range(16)]
    here = rhs3
    for _ in range(7):
        here = [
            sweep(
                here[x], roll(here[x], 1, 0), roll(here[x], -1, 0), here[(x + 15) % 16], here[(x + 1) % 16],
                roll(here[x], 1, 1), roll(here[x], -1, 1), rhs3[x], [terms3[q][x] for q in range(6)],
            )
            for x in range(16)
        ]

    wide = left(mat(8, 8, lambda i, j: j == (i >> 1)), jnp.concatenate([here[(X + 16) % 16] for X in range(-2, 3)], axis=1))
    wide = jnp.concatenate([wide[:, 128 * i : 128 * i + 128] for i in range(5)], axis=0)
    wide = right(wide, mat(128, 128, lambda i, j: (i == (j >> 1)) & (j < 96)))
    for x in range(2, 12):
        i = (x >> 1) - 1
        v2p[x] = v2p[x] + wide[8 * i : 8 * i + 8]
    for x in range(3, 11):
        v2q[x] = sweep_l(v2p, b2, c2, x)
    ups = [sweep_l(v2q, b2, c2, x) for x in range(4, 10)]

    wide = right(jnp.concatenate(ups, axis=0), mat(128, 128, lambda i, j: i == 16 + (j >> 1)))
    wide = left(mat(16, 8, lambda i, j: j == (i >> 1)), jnp.concatenate([wide[8 * i : 8 * i + 8] for i in range(6)], axis=1))
    for x in range(1, 11):
        i = x >> 1
        v1p[x] = v1p[x] + wide[:, 128 * i : 128 * i + 128]
    for x in range(2, 10):
        v1q[x] = sweep_l(v1p, b1, c1, x)
    ups = [sweep_l(v1q, b1, c1, x) for x in range(3, 9)]

    def lanes10(i, j):
        main = (j < 128) & (i == 32 + (j >> 1))
        return main | ((j >= 254) & (i == 31)) | ((j >= 128) & (j < 130) & (i == 96))

    def rows10(i, j):
        xi, zr = j >> 4, j & 15
        main = (i < 96) & (zr == (((i >> 4) + 15) & 15)) & (xi == 1 + ((i & 7) >> 1))
        n = i - 96
        beside = (i >= 96) & (zr == ((((n >> 3) + 31) >> 1) & 15)) & (
            (((n & 7) >= 6) & (xi == 0)) | (((n & 7) < 2) & (xi == 5))
        )
        return main | beside

    wide = right(jnp.concatenate(ups, axis=0), mat(128, 256, lanes10))
    wide = left(mat(176, 96, rows10), wide)
    wait(up0)
    low = (ly & 2) == 0
    beside = jnp.where(low, wpkr[0], wpkr[1])
    low_z = jnp.where(low, wpkr[2], wpkr[3])
    high_z = jnp.where(low, wpkr[4], wpkr[5])
    across = jnp.where(sx < 4, jnp.where(low, wpkr[8], wpkr[9]), jnp.where(low, wpkr[6], wpkr[7]))
    a = [wa[p] + wide[8 * p : 8 * p + 8, 0:128] for p in range(12)]
    x = [wx[p] + wide[96 + 8 * p : 104 + 8 * p, 0:128] for p in range(10)]
    y = []
    for p in range(10):
        if p == 0:
            base = roll(low_z, -30, 1)
        elif p == 9:
            base = roll(high_z, -2, 1)
        else:
            base = roll(beside, -(4 * (p - 1) + 2), 1)
        y.append(base + wide[8 * (p + 1) : 8 * (p + 1) + 8, 128:256])
    xy = [roll(across, -(4 * z + 2), 1) + wide[104 + 8 * z : 112 + 8 * z, 128:256] for z in range(8)]
    rim_sweep(a, x, y, xy)
    for z in range(8):
        out_ref[z] = sweep_a(va, vx, vy, 2 + z, 2)
    net.finish()


def on_device(source, decay_rate, dispersion, velocity, upwind):
    def vmem(*shape):
        return pltpu.VMEM(shape, F32)

    tile = (8, 128)
    scratch = [
        vmem(8, *tile), vmem(8, *tile), vmem(3, 8, *tile), vmem(3, 8, *tile), pltpu.VMEM((3, 8, *tile), jnp.int32),
        pltpu.SemaphoreType.DMA((5,)),
        vmem(3, 8, *tile), vmem(5, *tile), vmem(*tile), vmem(3, 8, *tile), vmem(3, *tile), vmem(2, *tile), vmem(*tile), vmem(*tile),
        vmem(7, 12, *tile), vmem(7, 10, *tile), vmem(7, 10, *tile), vmem(8, *tile), vmem(*tile), vmem(10, *tile),
        vmem(6, 8, *tile), vmem(8, *tile), vmem(12, *tile), vmem(8, *tile), vmem(8, *tile),
        vmem(12, *tile), vmem(10, *tile), vmem(*tile), vmem(10, *tile),
        vmem(7, 3, 2, 16, 128), vmem(2, *tile), vmem(3, 2, 16, 128), vmem(3, 2, 16, 128), vmem(3, 4, *tile), vmem(3, *tile),
        vmem(7, 12, 16, 128), vmem(7, 14, *tile), vmem(3, 16, *tile),
        vmem(3, 3, 2, 16, 128), vmem(12, 16, 128), vmem(12, 16, 128), vmem(12, 16, 128),
        vmem(14, *tile), vmem(2, *tile), vmem(14, *tile), vmem(14, *tile), vmem(14, *tile), vmem(14, *tile), vmem(14, *tile),
        vmem(16, *tile),
        pltpu.SemaphoreType.REGULAR, pltpu.SemaphoreType.REGULAR, pltpu.SemaphoreType.REGULAR,
        vmem(768, 128), pltpu.SemaphoreType.DMA((GROUPS,)), pltpu.SemaphoreType.DMA((GROUPS,)),
    ]
    return pl.pallas_call(
        kernel,
        out_shape=jax.ShapeDtypeStruct((8, 8, 128), F32),
        in_specs=[pl.BlockSpec(memory_space=pltpu.HBM)] * 5,
        out_specs=pl.BlockSpec(memory_space=pltpu.VMEM),
        scratch_shapes=scratch,
        compiler_params=pltpu.CompilerParams(collective_id=0, has_side_effects=True),
    )(source, decay_rate, dispersion, velocity, upwind)


def solution(mesh):
    field, vector = P("gz", "gx", "gy"), P(None, "gz", "gx", "gy")
    return jax.shard_map(
        on_device, mesh=mesh, in_specs=(field, field, vector, vector, vector), out_specs=field, check_vma=False
    )
```

```python
import jax
import jax.numpy as jnp
from jax import lax
from jax.experimental import pallas as pl
from jax.experimental.pallas import tpu as pltpu
from jax.sharding import PartitionSpec as P

MESH = pl.DeviceIdType.MESH
SIZES = (("gz", 4), ("gx", 16), ("gy", 8))
F32 = jnp.float32
RELAX = 0.7
KEEP = 1.0 - RELAX
GROUPS = 10

ZX = [(k, a) for k in range(4) for a in (0, 1, -1) if (k, a) != (0, 0)]


def hops(offset):
    return sum(min(step % size, -step % size) * (1 if size < 16 else 0.5) for (_, size), step in zip(SIZES, offset))


NEAR_27 = sorted(((k, a, t) for k, a in [(0, 0)] + ZX for t in (0, 1, -1)), key=hops, reverse=True)
ALONG_X = sorted(range(1, 16), key=lambda a: min(a, 16 - a), reverse=True)


class Net:
    def __init__(self, tally, send_sems, recv_sems):
        self.tally, self.send_sems, self.recv_sems = tally, send_sems, recv_sems
        self.rows, self.places = [], {}
        for name, size in SIZES:
            here = lax.axis_index(name)
            for step in range(size):
                self.places[name, step] = (here + step) & (size - 1) if step else here

    def at(self, offset):
        return {name: self.places[name, step % size] for (name, size), step in zip(SIZES, offset)}

    def signal(self, sem, offset):
        pl.semaphore_signal(sem, inc=1, device_id=self.at(offset), device_id_type=MESH)

    def group(self):
        self.rows.append(0)
        return len(self.rows) - 1

    def send(self, group, src, dst, offset):
        size = 1
        for n in src.shape:
            size *= n
        self.rows[group] += size // 128
        pltpu.make_async_remote_copy(
            src_ref=src,
            dst_ref=dst,
            send_sem=self.send_sems.at[group],
            recv_sem=self.recv_sems.at[group],
            device_id=self.at(offset),
            device_id_type=MESH,
        ).start()

    def whole(self, group):
        part = self.tally.at[pl.ds(0, self.rows[group])]
        return pltpu.make_async_remote_copy(
            src_ref=part,
            dst_ref=part,
            send_sem=self.send_sems.at[group],
            recv_sem=self.recv_sems.at[group],
            device_id=self.at((0, 0, 1)),
            device_id_type=MESH,
        )

    def wait(self, group):
        self.whole(group).wait_recv()

    def finish(self):
        for group in range(len(self.rows)):
            self.whole(group).wait_send()


def iota(shape, dim):
    return lax.broadcasted_iota(jnp.int32, shape, dim)


def mat(rows, cols, where):
    return jnp.where(where(iota((rows, cols), 0), iota((rows, cols), 1)), 1.0, 0.0).astype(F32)


def split(x):
    high = x.astype(jnp.bfloat16)
    return high, (x - high.astype(F32)).astype(jnp.bfloat16)


def dot(a, b, ones):
    if ones:
        b = b.astype(jnp.bfloat16)
        pairs = [(part, b) for part in split(a)]
    else:
        a = a.astype(jnp.bfloat16)
        pairs = [(a, part) for part in split(b)]
    high, low = [jnp.dot(x, y, preferred_element_type=F32) for x, y in pairs]
    return high + low


def left(a, b):
    return dot(a, b, 0)


def right(a, b):
    return dot(a, b, 1)


def roll(x, shift, axis):
    size = x.shape[axis]
    shift = shift % size
    return pltpu.roll(x, shift, axis) if shift else x


def low_lanes(i, parity):
    if parity is None:
        return i >= 0
    return (i & 1) == parity


PICKS = ((1, None, None), (0, None, None), (None, 1, None), (None, 0, None), (None, None, 1), (None, None, 0), (None, None, None))


def kernel(
    src_hbm, r_hbm, k_hbm, v_hbm, f_hbm, out_ref,
    src_ref, r_ref, k_ref, v_ref, f_ref, in_sems,
    e0a, e0z, e0y, xb0, zlo, zhi, ylo, yhi,
    ea, ex, ey, exy, pk, pkr,
    cu, d0, va, vx, vy,
    wa, wx, wpk, wpkr,
    p1, s1, s1l, s1h, a2, a3, c1, c2, c3,
    b1c, b1, v1p, v1q,
    b2c, b2r, b2l, b2h, b2, v2p, v2q,
    b3, go_a, go_b, go_c, tally, ssem, rsem,
):
    net = Net(tally, ssem, rsem)
    send, wait = net.send, net.wait
    gz, gx, gy = lax.axis_index("gz"), lax.axis_index("gx"), lax.axis_index("gy")
    sx, ly = iota((8, 128), 0), iota((8, 128), 1)

    fetches = [
        pltpu.make_async_copy(here, there, in_sems.at[i])
        for i, (here, there) in enumerate(
            ((k_hbm, k_ref), (v_hbm, v_ref), (f_hbm, f_ref), (src_hbm, src_ref), (r_hbm, r_ref))
        )
    ]
    for fetch in fetches:
        fetch.start()
    barrier = pltpu.get_barrier_semaphore()
    greeted = [(1, 0, 0), (2, 0, 0), (3, 0, 0), (0, 1, 0), (0, -1, 0), (0, 0, 1), (0, 0, -1)]
    for offset in greeted:
        net.signal(barrier, offset)

    for fetch in fetches[:3]:
        fetch.wait()
    e0a[0] = k_ref[1]
    e0a[1] = v_ref[1]
    e0a[2] = f_ref[1].astype(F32)
    e0z[0] = k_ref[0, 7]
    e0z[1] = v_ref[0, 7]
    e0z[2] = f_ref[0, 7].astype(F32)
    e0z[3] = k_ref[0, 0]
    e0z[4] = v_ref[0, 0]
    packed = jnp.zeros((8, 128), F32)
    for f, ref in enumerate((k_ref, v_ref, f_ref)):
        for z in range(8):
            start = 16 * f + 2 * z
            moved = roll(ref[2, z].astype(F32), start + 1, 1)
            packed = jnp.where((ly >= start) & (ly < start + 2), moved, packed)
    e0y[...] = packed
    pl.semaphore_wait(barrier, len(greeted))
    e0 = net.group()
    send(e0, e0a.at[:, :, pl.ds(7, 1), :], xb0.at[:, :, pl.ds(7, 1), :], (0, 1, 0))
    send(e0, e0a.at[pl.ds(0, 2), :, pl.ds(0, 1), :], xb0.at[pl.ds(0, 2), :, pl.ds(0, 1), :], (0, -1, 0))
    send(e0, e0z.at[pl.ds(0, 3)], zlo, (1, 0, 0))
    send(e0, e0z.at[pl.ds(3, 2)], zhi, (-1, 0, 0))
    send(e0, e0y, ylo, (0, 0, 1))
    send(e0, e0y, yhi, (0, 0, -1))

    def xprev(a, b):
        return roll(jnp.where(sx == 7, b, a), 1, 0)

    def xnext(a, b):
        return roll(jnp.where(sx == 0, b, a), -1, 0)

    def yprev(a, b):
        return roll(jnp.where(ly == 127, b, a), 1, 1)

    def ynext(a, b):
        return roll(jnp.where(ly == 0, b, a), -1, 1)

    wait(e0)
    for a in (2, -2):
        net.signal(go_a, (0, a, 0))
    for t in (1, -1):
        net.signal(go_c, (0, 0, t))
    for fetch in fetches[3:]:
        fetch.wait()

    both0 = jnp.where((ly & 1) == 0, ylo[...], yhi[...])
    pack = jnp.zeros((8, 128), F32)
    for z in range(8):
        k, v = [k_ref[d, z] for d in range(3)], [v_ref[d, z] for d in range(3)]
        f = [f_ref[d, z].astype(F32) for d in range(3)]
        side = [roll(both0, -(16 * q + 2 * z + 1), 1) for q in range(3)]
        kn = [
            k_ref[0, z + 1] if z < 7 else zhi[0],
            xnext(k[1], xb0[0, z]),
            ynext(k[2], side[0]),
        ]
        vn = [
            v_ref[0, z + 1] if z < 7 else zhi[1],
            xnext(v[1], xb0[1, z]),
            ynext(v[2], side[1]),
        ]
        kp = [
            k_ref[0, z - 1] if z else zlo[0],
            xprev(k[1], xb0[0, z]),
            yprev(k[2], side[0]),
        ]
        vp = [
            v_ref[0, z - 1] if z else zlo[1],
            xprev(v[1], xb0[1, z]),
            yprev(v[2], side[1]),
        ]
        fp = [
            f_ref[0, z - 1].astype(F32) if z else zlo[2],
            xprev(f[1], xb0[2, z]),
            yprev(f[2], side[2]),
        ]
        last = [
            (gz == 3) if z == 7 else None,
            (sx == 7) & (gx == 15),
            (ly == 127) & (gy == 7),
        ]
        first = [
            (gz == 0) if z == 0 else None,
            (sx == 0) & (gx == 0),
            (ly == 0) & (gy == 0),
        ]
        terms = []
        for d in range(3):
            up = 0.5 * (k[d] + kn[d]) + f[d] * (0.5 * (v[d] + vn[d]))
            down = 0.5 * (kp[d] + k[d]) + (1.0 - fp[d]) * (0.5 * (vp[d] + v[d]))
            if last[d] is not None:
                up = jnp.where(last[d], 0.0, up)
            if first[d] is not None:
                down = jnp.where(first[d], 0.0, down)
            terms += [up, down]
        rate = r_ref[z]
        diag = rate
        for term in terms:
            diag = diag + term
        scale = RELAX / diag
        d0[z] = diag * (1.0 / RELAX)
        for q in range(6):
            cu[q, z] = terms[q]
            scaled = terms[q] * scale
            ea[1 + q, 2 + z] = scaled
            start = 32 + 16 * q + 2 * z
            pack = jnp.where((ly >= start) & (ly < start + 2), roll(scaled, start + 1, 1), pack)
        begun = src_ref[z] * scale
        ea[0, 2 + z] = begun
        pack = jnp.where((ly >= 4 * z) & (ly < 4 * z + 4), roll(begun, 4 * z + 2, 1), pack)
    pk[...] = pack

    diagonal_y = [(0, 0, 1), (0, 0, -1)] + [(s, 0, t) for s in (1, -1) for t in (1, -1)] + [(0, s, t) for s in (1, -1) for t in (1, -1)]

    def rim(group, a, x, p, pr):
        for s in (1, -1):
            mine, theirs = (8, 0) if s == 1 else (2, 10)
            send(group, a.at[pl.ds(mine, 2)], a.at[pl.ds(theirs, 2)], (s, 0, 0))
            row = 6 if s == 1 else 0
            send(group, a.at[pl.ds(2, 8), pl.ds(row, 2)], x.at[pl.ds(1, 8), pl.ds(row, 2)], (0, s, 0))
        for i, offset in enumerate(diagonal_y):
            send(group, p, pr.at[i], offset)
        for s in (1, -1):
            for t in (1, -1):
                plane, row = (9 if s == 1 else 2), (7 if t == 1 else 0)
                there = x.at[pl.ds(0 if s == 1 else 9, 1), pl.ds(row, 1)]
                send(group, a.at[pl.ds(plane, 1), pl.ds(row, 1)], there, (s, t, 0))

    r1 = net.group()
    for s in (1, -1):
        mine, theirs, row = (9, 1, 7) if s == 1 else (2, 10, 0)
        send(r1, ea.at[pl.ds(1, 6), pl.ds(mine, 1)], ea.at[pl.ds(1, 6), pl.ds(theirs, 1)], (s, 0, 0))
        there = ex.at[pl.ds(1, 6), pl.ds(1, 8), pl.ds(row, 1)]
        send(r1, ea.at[pl.ds(1, 6), pl.ds(2, 8), pl.ds(row, 1)], there, (0, s, 0))
    rim(r1, ea.at[0], ex.at[0], pk, pkr)

    own1 = (iota((16, 128), 1) >= 32) & (iota((16, 128), 1) < 96)

    def scaled_terms(fields, inside):
        diag = fields[6]
        for q in range(6):
            diag = diag + fields[q]
        diag = jnp.where(inside, diag, 1.0)
        scale = jnp.where(inside, RELAX / diag, 0.0)
        return [fields[q] * scale for q in range(6)] + [jnp.where(inside, diag * (1.0 / RELAX), 0.0)]

    def pairs(q, a, b):
        pick = PICKS[q][0]
        return a + b if pick is None else (b if pick else a)

    def lanes01(pick):
        return mat(128, 128, lambda i, j: (j == 32 + (i >> 1)) & low_lanes(i, pick))

    def lanes12(pick):
        return mat(128, 128, lambda i, j: (j == 16 + (i >> 1)) & (i >= 32) & (i < 96) & low_lanes(i, pick))

    def lanes23(pick):
        return mat(128, 128, lambda i, j: (j == (i >> 1)) & (i >= 32) & (i < 64) & low_lanes(i, pick))

    def rows01(pick):
        return mat(16, 32, lambda i, j: ((j >> 3) == (i & 3)) & (((j & 7) >> 1) == (i >> 2)) & low_lanes(j, pick))

    def rows12(pz, px):
        return mat(
            8, 16,
            lambda i, j: ((j >> 3) == (i >> 1)) & (((j & 3) >> 1) == (i & 1)) & low_lanes(j, pz) & low_lanes(j >> 2, px),
        )

    def rows23(pz, px):
        return mat(8, 8, lambda i, j: (i == 0) & (j < 4) & low_lanes(j, pz) & low_lanes(j >> 1, px))

    def halves(block):
        return jnp.where(own8, block[0:8], roll(block[8:16], 64, 1))

    def zslot(k):
        return (4 - k) % 4

    def xplace(own, per, a):
        return own - per * a

    own8 = (ly >= 32) & (ly < 96)
    level1 = []
    for q in range(7):
        planes = [pairs(q, (cu[q, 2 * z] if q < 6 else r_ref[2 * z]), (cu[q, 2 * z + 1] if q < 6 else r_ref[2 * z + 1])) for z in range(4)]
        stacked = jnp.concatenate(planes, axis=0)
        level1.append(right(left(rows01(PICKS[q][1]), stacked), lanes01(PICKS[q][2])))
    scaled1 = scaled_terms(level1, own1)
    d1_own = scaled1[6]
    strip = jnp.zeros((8, 128), F32)
    for q in range(7):
        block = halves(scaled1[q])
        for x in range(2):
            p1[q, 1, x, 0:4, :] = block[4 * x : 4 * x + 4]
        if q < 6:
            for h in range(2):
                t = 4 * (2 * q + h)
                moved = roll(scaled1[q][8 * h : 8 * h + 8], t - 92, 1)
                strip = jnp.where(((ly >= t) & (ly < t + 4)) | ((ly >= t + 68) & (ly < t + 72)), moved, strip)
    for x in range(2):
        s1[x, 0:4, :] = strip[4 * x : 4 * x + 4]
    c1_copies = net.group()
    for k, a in ZX:
        n = 6 if a else 7
        there = p1.at[pl.ds(0, n), pl.ds(1 - a, 1), :, pl.ds(4 * zslot(k), 4)]
        send(c1_copies, p1.at[pl.ds(0, n), pl.ds(1, 1), :, pl.ds(0, 4)], there, (k, a, 0))
    level2 = [right(left(rows12(PICKS[q][0], PICKS[q][1]), level1[q]), lanes12(PICKS[q][2])) for q in range(7)]
    level3 = [right(left(rows23(PICKS[q][0], PICKS[q][1]), level2[q]), lanes23(PICKS[q][2])) for q in range(7)]
    inside2 = (ly >= 32) & (ly < 64) & (sx < 4)
    inside3 = (ly >= 16) & (ly < 32) & (sx < 1)
    scaled2 = scaled_terms(level2, inside2)
    scaled3 = scaled_terms(level3, inside3)
    group = [jnp.zeros((8, 128), F32), jnp.zeros((8, 128), F32)]
    line = jnp.zeros((8, 128), F32)
    for q in range(7):
        g, j = q // 4, q % 4
        group[g] = group[g] + roll(scaled2[q], 32 * j - 32, 1)
        line = line + roll(scaled3[q], 16 * q - 16, 1)
    for g in range(2):
        for x in range(2):
            a2[1, 2 * g + x, 0:2, :] = group[g][2 * x : 2 * x + 2]
    a3[1, 0:1, :] = line[0:1]
    z_copies = net.group()
    for k in range(4):
        for t in (0, 1, -1):
            if k or t:
                there = a2.at[pl.ds(1 - t, 1), :, pl.ds(2 * zslot(k), 2)]
                send(z_copies, a2.at[pl.ds(1, 1), :, pl.ds(0, 2)], there, (k, 0, t))
                send(z_copies, a3.at[pl.ds(1, 1), pl.ds(0, 1)], a3.at[pl.ds(1 - t, 1), pl.ds(zslot(k), 1)], (k, 0, t))

    wait(r1)
    pl.semaphore_wait(go_a, 2)
    for a in (4, -4):
        net.signal(go_b, (0, a, 0))

    def unpack(pr, y, xy):
        from_low = (ly & jnp.where(ly < 32, 2, 1)) == 0

        def both(low, high):
            return jnp.where(from_low, pr[low], pr[high])

        beside = both(0, 1)
        for z in range(8):
            y[1 + z] = roll(beside, -(4 * z + 2), 1)
        y[0] = roll(both(2, 3), -30, 1)
        y[9] = roll(both(4, 5), -2, 1)
        across = jnp.where(sx < 4, both(8, 9), both(6, 7))
        for z in range(8):
            xy[z] = roll(across, -(4 * z + 2), 1)
        return beside

    beside = unpack(pkr, ey.at[0], exy)
    for q in range(6):
        for z in range(8):
            ey[1 + q, 1 + z] = roll(beside, -(32 + 16 * q + 2 * z + 1), 1)

    def sweep(here, zp, zn, xp, xn, yp, yn, rhs, s):
        total = KEEP * here + rhs
        total = total + s[0] * zn + s[1] * zp
        total = total + s[2] * xn + s[3] * xp
        return total + s[4] * yn + s[5] * yp

    def sweep_a(a, x, y, p, outer):
        here = a[p]
        bx, by = x[p - outer], y[p - outer]
        return sweep(
            here, a[p - 1], a[p + 1], xprev(here, bx), xnext(here, bx), yprev(here, by), ynext(here, by),
            ea[0, p], [ea[1 + q, p] for q in range(6)],
        )

    def rim_sweep(a, x, y, xy):
        for p in range(1, 11):
            va[p] = sweep_a(a, x, y, p, 1)
        for z in range(8):
            here = x[1 + z]
            ba, bxy = a[2 + z], xy[z]
            vx[z] = sweep(
                here, x[z], x[2 + z], xprev(here, ba), xnext(here, ba), yprev(here, bxy), ynext(here, bxy),
                ex[0, 1 + z], [ex[1 + q, 1 + z] for q in range(6)],
            )
            here = y[1 + z]
            vy[z] = sweep(
                here, y[z], y[2 + z], xprev(here, bxy), xnext(here, bxy), yprev(here, ba), ynext(here, ba),
                ey[0, 1 + z], [ey[1 + q, 1 + z] for q in range(6)],
            )

    rim_sweep(ea.at[0], ex.at[0], ey.at[0], exy)
    planes = []
    for z in range(4):
        two = [(sweep_a(va, vx, vy, 2 + p, 2) - va[2 + p]) * d0[p] for p in (2 * z, 2 * z + 1)]
        planes.append(two[0] + two[1])
    rhs1 = right(left(rows01(None), jnp.concatenate(planes, axis=0)), lanes01(None))
    rhs1 = halves(jnp.where(own1, rhs1 / jnp.where(own1, d1_own, 1.0), 0.0))
    for x in range(2):
        b1c[1, 1, x, 0:4, :] = rhs1[4 * x : 4 * x + 4]

    r2 = net.group()
    for k, a, t in NEAR_27:
        if (k, a, t) != (0, 0, 0):
            there = b1c.at[1 - t, 1 - a, :, pl.ds(4 * zslot(k), 4)]
            send(r2, b1c.at[1, 1, :, pl.ds(0, 4)], there, (k, a, t))

    pl.semaphore_wait(go_c, 2)
    for k, a in [(0, 0)] + ZX:
        for t in (1, -1):
            there = s1l if t == 1 else s1h
            send(c1_copies, s1.at[:, pl.ds(0, 4)], there.at[1 - a, :, pl.ds(4 * zslot(k), 4)], (k, a, t))

    pack = jnp.zeros((8, 128), F32)
    for z in range(8):
        plane = va[2 + z]
        wa[2 + z] = plane
        pack = jnp.where((ly >= 4 * z) & (ly < 4 * z + 4), roll(plane, 4 * z + 2, 1), pack)
    wpk[...] = pack
    up0 = net.group()
    rim(up0, wa, wx, wpk, wpkr)

    wait(z_copies)
    for q in range(7):
        g, j = q // 4, q % 4
        for x in range(2):
            low, mid, high = [roll(a2[t, 2 * g + x], 32 * t - 32 * j, 1) for t in range(3)]
            c2[q, 6 + x] = jnp.where(ly < 32, low, jnp.where(ly < 64, mid, jnp.where(ly < 96, high, 0.0)))
    c2_copies = net.group()
    for a in (1, -1, 2, -2, 3, -3):
        send(c2_copies, c2.at[pl.ds(0, 6), pl.ds(6, 2)], c2.at[pl.ds(0, 6), pl.ds(xplace(6, 2, a), 2)], (0, a, 0))
    fields3 = []
    for q in range(7):
        low, mid, high = [roll(a3[t], 16 * t - 16 * q, 1) for t in range(3)]
        fields3.append(jnp.where(ly < 16, low, jnp.where(ly < 32, mid, jnp.where(ly < 48, high, 0.0))))
    for q in range(3):
        c3[q, 0] = jnp.where(ly < 64, fields3[2 * q], roll(fields3[2 * q + 1], 64, 1))

    def sweep_l(v, b, c, x):
        here = v[x]
        return sweep(
            here, roll(here, 1, 0), roll(here, -1, 0), v[x - 1], v[x + 1], roll(here, 1, 1), roll(here, -1, 1),
            b[x], [c[q, x] for q in range(6)],
        )

    wait(c1_copies)
    lane16 = iota((16, 128), 1)
    own16 = (lane16 >= 32) & (lane16 < 96)
    for i in range(3):
        for x in range(2):
            rims = jnp.where(lane16 < 64, s1l[i, x], s1h[i, x])
            for q in range(6):
                block = p1[q, i, x]
                c1[q, 4 * i + x] = jnp.where(own16, block, roll(rims, 28 - 8 * q, 1))
                c1[q, 4 * i + 2 + x] = jnp.where(own16, roll(block, 64, 1), roll(rims, 24 - 8 * q, 1))
    for x in range(2):
        block = p1[6, 1, x]
        c1[6, 4 + x] = block
        c1[6, 6 + x] = roll(block, 64, 1)
    wait(r2)
    for i in range(3):
        for x in range(2):
            low, mid, high = [b1c[t, i, x] for t in range(3)]
            b1[4 * i + x] = jnp.where(own16, mid, roll(jnp.where(lane16 >= 64, low, high), 64, 1))
            b1[4 * i + 2 + x] = jnp.where(own16, roll(mid, 64, 1), jnp.where(lane16 < 64, low, high))
    for x in range(1, 11):
        v1p[x] = sweep_l(b1, b1, c1, x)
    rows = []
    for x in range(2):
        two = [(sweep_l(v1p, b1, c1, p) - v1p[p]) * c1[6, p] for p in (4 + 2 * x, 5 + 2 * x)]
        rows.append(two[0] + two[1])
    rows = right(jnp.concatenate(rows, axis=0), lanes12(None))
    halve = mat(8, 16, lambda i, j: (j >> 1) == i)
    for x in range(2):
        inside = (ly >= 32) & (ly < 64)
        rhs2 = left(halve, rows[16 * x : 16 * x + 16])
        rhs2 = jnp.where(inside, rhs2 / jnp.where(inside, c2[6, 6 + x], 1.0), 0.0)
        b2c[6 + x] = rhs2
        b2r[x] = roll(rhs2, 32, 1) + roll(rhs2, -32, 1)

    r3 = net.group()
    for a in (3, -3, 2, -2, 1, -1, 0):
        there = pl.ds(xplace(6, 2, a), 2)
        send(r3, b2r, b2l.at[there], (0, a, 1))
        send(r3, b2r, b2h.at[there], (0, a, -1))
    for a in (3, -3, 2, -2, 1, -1):
        send(r3, b2c.at[pl.ds(6, 2)], b2c.at[pl.ds(xplace(6, 2, a), 2)], (0, a, 0))
    pl.semaphore_wait(go_b, 2)
    c3_copies = net.group()
    for a in range(1, 16):
        send(c3_copies, c3.at[:, pl.ds(0, 1), pl.ds(0, 4)], c3.at[:, pl.ds(16 - a, 1), pl.ds(0, 4)], (0, a, 0))

    wait(c2_copies)
    wait(r3)
    for x in range(14):
        b2[x] = jnp.where(ly < 32, b2l[x], jnp.where(ly >= 64, b2h[x], b2c[x]))
    for x in range(2, 12):
        v2p[x] = sweep_l(b2, b2, c2, x)
    two = [(sweep_l(v2p, b2, c2, p) - v2p[p]) * c2[6, p] for p in (6, 7)]
    rows = right(two[0] + two[1], mat(128, 128, lambda i, j: (j == (i >> 1)) & (i < 96)))
    rhs3 = left(mat(8, 8, lambda i, j: (j >> 1) == (i & 3)), rows)

    def twice(block):
        return jnp.where(sx < 4, block, roll(block, 4, 0))

    inside = ly < 48
    rhs3 = jnp.where(inside, rhs3 / jnp.where(inside, twice(fields3[6]), 1.0), 0.0)
    b3[0] = rhs3

    r4 = net.group()
    for a in ALONG_X:
        send(r4, b3.at[pl.ds(0, 1)], b3.at[pl.ds(16 - a, 1)], (0, a, 0))
    wait(c3_copies)
    terms3 = []
    for q in range(3):
        terms3.append([twice(c3[q, x]) for x in range(16)])
        terms3.append([roll(block, 64, 1) for block in terms3[-1]])
    wait(r4)
    rhs3 = [b3[x] for x in range(16)]
    here = rhs3
    for _ in range(7):
        here = [
            sweep(
                here[x], roll(here[x], 1, 0), roll(here[x], -1, 0), here[(x + 15) % 16], here[(x + 1) % 16],
                roll(here[x], 1, 1), roll(here[x], -1, 1), rhs3[x], [terms3[q][x] for q in range(6)],
            )
            for x in range(16)
        ]

    wide = left(mat(8, 8, lambda i, j: j == (i >> 1)), jnp.concatenate([here[(X + 16) % 16] for X in range(-2, 3)], axis=1))
    wide = jnp.concatenate([wide[:, 128 * i : 128 * i + 128] for i in range(5)], axis=0)
    wide = right(wide, mat(128, 128, lambda i, j: (i == (j >> 1)) & (j < 96)))
    for x in range(2, 12):
        i = (x >> 1) - 1
        v2p[x] = v2p[x] + wide[8 * i : 8 * i + 8]
    for x in range(3, 11):
        v2q[x] = sweep_l(v2p, b2, c2, x)
    ups = [sweep_l(v2q, b2, c2, x) for x in range(4, 10)]

    wide = right(jnp.concatenate(ups, axis=0), mat(128, 128, lambda i, j: i == 16 + (j >> 1)))
    wide = left(mat(16, 8, lambda i, j: j == (i >> 1)), jnp.concatenate([wide[8 * i : 8 * i + 8] for i in range(6)], axis=1))
    for x in range(1, 11):
        i = x >> 1
        v1p[x] = v1p[x] + wide[:, 128 * i : 128 * i + 128]
    for x in range(2, 10):
        v1q[x] = sweep_l(v1p, b1, c1, x)
    ups = [sweep_l(v1q, b1, c1, x) for x in range(3, 9)]

    def lanes10(i, j):
        main = (j < 128) & (i == 32 + (j >> 1))
        return main | ((j >= 254) & (i == 31)) | ((j >= 128) & (j < 130) & (i == 96))

    def rows10(i, j):
        xi, zr = j >> 4, j & 15
        main = (i < 96) & (zr == (((i >> 4) + 15) & 15)) & (xi == 1 + ((i & 7) >> 1))
        n = i - 96
        beside = (i >= 96) & (zr == ((((n >> 3) + 31) >> 1) & 15)) & (
            (((n & 7) >= 6) & (xi == 0)) | (((n & 7) < 2) & (xi == 5))
        )
        return main | beside

    wide = right(jnp.concatenate(ups, axis=0), mat(128, 256, lanes10))
    wide = left(mat(176, 96, rows10), wide)
    wait(up0)
    low = (ly & 2) == 0
    beside = jnp.where(low, wpkr[0], wpkr[1])
    low_z = jnp.where(low, wpkr[2], wpkr[3])
    high_z = jnp.where(low, wpkr[4], wpkr[5])
    across = jnp.where(sx < 4, jnp.where(low, wpkr[8], wpkr[9]), jnp.where(low, wpkr[6], wpkr[7]))
    a = [wa[p] + wide[8 * p : 8 * p + 8, 0:128] for p in range(12)]
    x = [wx[p] + wide[96 + 8 * p : 104 + 8 * p, 0:128] for p in range(10)]
    y = []
    for p in range(10):
        if p == 0:
            base = roll(low_z, -30, 1)
        elif p == 9:
            base = roll(high_z, -2, 1)
        else:
            base = roll(beside, -(4 * (p - 1) + 2), 1)
        y.append(base + wide[8 * (p + 1) : 8 * (p + 1) + 8, 128:256])
    xy = [roll(across, -(4 * z + 2), 1) + wide[104 + 8 * z : 112 + 8 * z, 128:256] for z in range(8)]
    rim_sweep(a, x, y, xy)
    for z in range(8):
        out_ref[z] = sweep_a(va, vx, vy, 2 + z, 2)
    net.finish()


def on_device(source, decay_rate, dispersion, velocity, upwind):
    def vmem(*shape):
        return pltpu.VMEM(shape, F32)

    tile = (8, 128)
    scratch = [
        vmem(8, *tile), vmem(8, *tile), vmem(3, 8, *tile), vmem(3, 8, *tile), pltpu.VMEM((3, 8, *tile), jnp.int32),
        pltpu.SemaphoreType.DMA((5,)),
        vmem(3, 8, *tile), vmem(5, *tile), vmem(*tile), vmem(3, 8, *tile), vmem(3, *tile), vmem(2, *tile), vmem(*tile), vmem(*tile),
        vmem(7, 12, *tile), vmem(7, 10, *tile), vmem(7, 10, *tile), vmem(8, *tile), vmem(*tile), vmem(10, *tile),
        vmem(6, 8, *tile), vmem(8, *tile), vmem(12, *tile), vmem(8, *tile), vmem(8, *tile),
        vmem(12, *tile), vmem(10, *tile), vmem(*tile), vmem(10, *tile),
        vmem(7, 3, 2, 16, 128), vmem(2, *tile), vmem(3, 2, 16, 128), vmem(3, 2, 16, 128), vmem(3, 4, *tile), vmem(3, *tile),
        vmem(7, 12, 16, 128), vmem(7, 14, *tile), vmem(3, 16, *tile),
        vmem(3, 3, 2, 16, 128), vmem(12, 16, 128), vmem(12, 16, 128), vmem(12, 16, 128),
        vmem(14, *tile), vmem(2, *tile), vmem(14, *tile), vmem(14, *tile), vmem(14, *tile), vmem(14, *tile), vmem(14, *tile),
        vmem(16, *tile),
        pltpu.SemaphoreType.REGULAR, pltpu.SemaphoreType.REGULAR, pltpu.SemaphoreType.REGULAR,
        vmem(768, 128), pltpu.SemaphoreType.DMA((GROUPS,)), pltpu.SemaphoreType.DMA((GROUPS,)),
    ]
    return pl.pallas_call(
        kernel,
        out_shape=jax.ShapeDtypeStruct((8, 8, 128), F32),
        in_specs=[pl.BlockSpec(memory_space=pltpu.HBM)] * 5,
        out_specs=pl.BlockSpec(memory_space=pltpu.VMEM),
        scratch_shapes=scratch,
        compiler_params=pltpu.CompilerParams(collective_id=0, has_side_effects=True),
    )(source, decay_rate, dispersion, velocity, upwind)


def solution(mesh):
    field, vector = P("gz", "gx", "gy"), P(None, "gz", "gx", "gy")
    return jax.shard_map(
        on_device, mesh=mesh, in_specs=(field, field, vector, vector, vector), out_specs=field, check_vma=False
    )
```

```python
import jax
import jax.numpy as jnp
from jax import lax
from jax.experimental import pallas as pl
from jax.experimental.pallas import tpu as pltpu
from jax.sharding import PartitionSpec as P

MESH = pl.DeviceIdType.MESH
SIZES = (("gz", 4), ("gx", 16), ("gy", 8))
F32 = jnp.float32
RELAX = 0.7
KEEP = 1.0 - RELAX
GROUPS = 10

ZX = [(k, a) for k in range(4) for a in (0, 1, -1) if (k, a) != (0, 0)]


def hops(offset):
    return sum(min(step % size, -step % size) * (1 if size < 16 else 0.5) for (_, size), step in zip(SIZES, offset))


NEAR_27 = sorted(((k, a, t) for k, a in [(0, 0)] + ZX for t in (0, 1, -1)), key=hops, reverse=True)
ALONG_X = sorted(range(1, 16), key=lambda a: min(a, 16 - a), reverse=True)


class Net:
    def __init__(self, tally, send_sems, recv_sems):
        self.tally, self.send_sems, self.recv_sems = tally, send_sems, recv_sems
        self.rows, self.places = [], {}
        for name, size in SIZES:
            here = lax.axis_index(name)
            for step in range(size):
                self.places[name, step] = (here + step) & (size - 1) if step else here

    def at(self, offset):
        return {name: self.places[name, step % size] for (name, size), step in zip(SIZES, offset)}

    def signal(self, sem, offset):
        pl.semaphore_signal(sem, inc=1, device_id=self.at(offset), device_id_type=MESH)

    def group(self):
        self.rows.append(0)
        return len(self.rows) - 1

    def send(self, group, src, dst, offset):
        size = 1
        for n in src.shape:
            size *= n
        self.rows[group] += size // 128
        pltpu.make_async_remote_copy(
            src_ref=src,
            dst_ref=dst,
            send_sem=self.send_sems.at[group],
            recv_sem=self.recv_sems.at[group],
            device_id=self.at(offset),
            device_id_type=MESH,
        ).start()

    def whole(self, group):
        part = self.tally.at[pl.ds(0, self.rows[group])]
        return pltpu.make_async_remote_copy(
            src_ref=part,
            dst_ref=part,
            send_sem=self.send_sems.at[group],
            recv_sem=self.recv_sems.at[group],
            device_id=self.at((0, 0, 1)),
            device_id_type=MESH,
        )

    def wait(self, group):
        self.whole(group).wait_recv()

    def finish(self):
        for group in range(len(self.rows)):
            self.whole(group).wait_send()


def iota(shape, dim):
    return lax.broadcasted_iota(jnp.int32, shape, dim)


def mat(rows, cols, where):
    return jnp.where(where(iota((rows, cols), 0), iota((rows, cols), 1)), 1.0, 0.0).astype(jnp.bfloat16)


def split(x):
    high = x.astype(jnp.bfloat16)
    return high, (x - high.astype(F32)).astype(jnp.bfloat16)


def dot(a, b, ones):
    if ones:
        b = b.astype(jnp.bfloat16)
        pairs = [(part, b) for part in split(a)]
    else:
        a = a.astype(jnp.bfloat16)
        pairs = [(a, part) for part in split(b)]
    high, low = [jnp.dot(x, y, preferred_element_type=F32) for x, y in pairs]
    return high + low


def left(a, b):
    return dot(a, b, 0)


def right(a, b):
    return dot(a, b, 1)


def roll(x, shift, axis):
    size = x.shape[axis]
    shift = shift % size
    return pltpu.roll(x, shift, axis) if shift else x


def low_lanes(i, parity):
    if parity is None:
        return i >= 0
    return (i & 1) == parity


PICKS = ((1, None, None), (0, None, None), (None, 1, None), (None, 0, None), (None, None, 1), (None, None, 0), (None, None, None))


def kernel(
    src_hbm, r_hbm, k_hbm, v_hbm, f_hbm, out_ref,
    src_ref, r_ref, k_ref, v_ref, f_ref, in_sems,
    e0a, e0z, e0y, xb0, zlo, zhi, ylo, yhi,
    ea, ex, ey, exy, pk, pkr,
    cu, d0, va, vx, vy,
    wa, wx, wpk, wpkr,
    p1, s1, s1l, s1h, a2, a3, c1, c2, c3,
    b1c, b1, v1p, v1q,
    b2c, b2r, b2l, b2h, b2, v2p, v2q,
    b3, go_a, go_b, go_c, tally, ssem, rsem,
):
    net = Net(tally, ssem, rsem)
    send, wait = net.send, net.wait
    gz, gx, gy = lax.axis_index("gz"), lax.axis_index("gx"), lax.axis_index("gy")
    sx, ly = iota((8, 128), 0), iota((8, 128), 1)

    fetches = [
        pltpu.make_async_copy(here, there, in_sems.at[i])
        for i, (here, there) in enumerate(
            ((k_hbm, k_ref), (v_hbm, v_ref), (f_hbm, f_ref), (src_hbm, src_ref), (r_hbm, r_ref))
        )
    ]
    for fetch in fetches:
        fetch.start()
    barrier = pltpu.get_barrier_semaphore()
    greeted = [(1, 0, 0), (2, 0, 0), (3, 0, 0), (0, 1, 0), (0, -1, 0), (0, 0, 1), (0, 0, -1)]
    for offset in greeted:
        net.signal(barrier, offset)

    for fetch in fetches[:3]:
        fetch.wait()
    e0a[0] = k_ref[1]
    e0a[1] = v_ref[1]
    e0a[2] = f_ref[1].astype(F32)
    e0z[0] = k_ref[0, 7]
    e0z[1] = v_ref[0, 7]
    e0z[2] = f_ref[0, 7].astype(F32)
    e0z[3] = k_ref[0, 0]
    e0z[4] = v_ref[0, 0]
    packed = jnp.zeros((8, 128), F32)
    for f, ref in enumerate((k_ref, v_ref, f_ref)):
        for z in range(8):
            start = 16 * f + 2 * z
            moved = roll(ref[2, z].astype(F32), start + 1, 1)
            packed = jnp.where((ly >= start) & (ly < start + 2), moved, packed)
    e0y[...] = packed
    pl.semaphore_wait(barrier, len(greeted))
    e0 = net.group()
    send(e0, e0a.at[:, :, pl.ds(7, 1), :], xb0.at[:, :, pl.ds(7, 1), :], (0, 1, 0))
    send(e0, e0a.at[pl.ds(0, 2), :, pl.ds(0, 1), :], xb0.at[pl.ds(0, 2), :, pl.ds(0, 1), :], (0, -1, 0))
    send(e0, e0z.at[pl.ds(0, 3)], zlo, (1, 0, 0))
    send(e0, e0z.at[pl.ds(3, 2)], zhi, (-1, 0, 0))
    send(e0, e0y, ylo, (0, 0, 1))
    send(e0, e0y, yhi, (0, 0, -1))

    def xprev(a, b):
        return roll(jnp.where(sx == 7, b, a), 1, 0)

    def xnext(a, b):
        return roll(jnp.where(sx == 0, b, a), -1, 0)

    def yprev(a, b):
        return roll(jnp.where(ly == 127, b, a), 1, 1)

    def ynext(a, b):
        return roll(jnp.where(ly == 0, b, a), -1, 1)

    wait(e0)
    for a in (2, -2):
        net.signal(go_a, (0, a, 0))
    for t in (1, -1):
        net.signal(go_c, (0, 0, t))
    for fetch in fetches[3:]:
        fetch.wait()

    both0 = jnp.where((ly & 1) == 0, ylo[...], yhi[...])
    pack = jnp.zeros((8, 128), F32)
    for z in range(8):
        k, v = [k_ref[d, z] for d in range(3)], [v_ref[d, z] for d in range(3)]
        f = [f_ref[d, z].astype(F32) for d in range(3)]
        side = [roll(both0, -(16 * q + 2 * z + 1), 1) for q in range(3)]
        kn = [
            k_ref[0, z + 1] if z < 7 else zhi[0],
            xnext(k[1], xb0[0, z]),
            ynext(k[2], side[0]),
        ]
        vn = [
            v_ref[0, z + 1] if z < 7 else zhi[1],
            xnext(v[1], xb0[1, z]),
            ynext(v[2], side[1]),
        ]
        kp = [
            k_ref[0, z - 1] if z else zlo[0],
            xprev(k[1], xb0[0, z]),
            yprev(k[2], side[0]),
        ]
        vp = [
            v_ref[0, z - 1] if z else zlo[1],
            xprev(v[1], xb0[1, z]),
            yprev(v[2], side[1]),
        ]
        fp = [
            f_ref[0, z - 1].astype(F32) if z else zlo[2],
            xprev(f[1], xb0[2, z]),
            yprev(f[2], side[2]),
        ]
        last = [
            (gz == 3) if z == 7 else None,
            (sx == 7) & (gx == 15),
            (ly == 127) & (gy == 7),
        ]
        first = [
            (gz == 0) if z == 0 else None,
            (sx == 0) & (gx == 0),
            (ly == 0) & (gy == 0),
        ]
        terms = []
        for d in range(3):
            up = 0.5 * (k[d] + kn[d]) + f[d] * (0.5 * (v[d] + vn[d]))
            down = 0.5 * (kp[d] + k[d]) + (1.0 - fp[d]) * (0.5 * (vp[d] + v[d]))
            if last[d] is not None:
                up = jnp.where(last[d], 0.0, up)
            if first[d] is not None:
                down = jnp.where(first[d], 0.0, down)
            terms += [up, down]
        rate = r_ref[z]
        diag = rate
        for term in terms:
            diag = diag + term
        scale = RELAX / diag
        d0[z] = diag * (1.0 / RELAX)
        for q in range(6):
            cu[q, z] = terms[q]
            scaled = terms[q] * scale
            ea[1 + q, 2 + z] = scaled
            start = 32 + 16 * q + 2 * z
            pack = jnp.where((ly >= start) & (ly < start + 2), roll(scaled, start + 1, 1), pack)
        begun = src_ref[z] * scale
        ea[0, 2 + z] = begun
        pack = jnp.where((ly >= 4 * z) & (ly < 4 * z + 4), roll(begun, 4 * z + 2, 1), pack)
    pk[...] = pack

    diagonal_y = [(0, 0, 1), (0, 0, -1)] + [(s, 0, t) for s in (1, -1) for t in (1, -1)] + [(0, s, t) for s in (1, -1) for t in (1, -1)]

    def rim(group, a, x, p, pr):
        for s in (1, -1):
            mine, theirs = (8, 0) if s == 1 else (2, 10)
            send(group, a.at[pl.ds(mine, 2)], a.at[pl.ds(theirs, 2)], (s, 0, 0))
            row = 6 if s == 1 else 0
            send(group, a.at[pl.ds(2, 8), pl.ds(row, 2)], x.at[pl.ds(1, 8), pl.ds(row, 2)], (0, s, 0))
        for i, offset in enumerate(diagonal_y):
            send(group, p, pr.at[i], offset)
        for s in (1, -1):
            for t in (1, -1):
                plane, row = (9 if s == 1 else 2), (7 if t == 1 else 0)
                there = x.at[pl.ds(0 if s == 1 else 9, 1), pl.ds(row, 1)]
                send(group, a.at[pl.ds(plane, 1), pl.ds(row, 1)], there, (s, t, 0))

    r1 = net.group()
    for s in (1, -1):
        mine, theirs, row = (9, 1, 7) if s == 1 else (2, 10, 0)
        send(r1, ea.at[pl.ds(1, 6), pl.ds(mine, 1)], ea.at[pl.ds(1, 6), pl.ds(theirs, 1)], (s, 0, 0))
        there = ex.at[pl.ds(1, 6), pl.ds(1, 8), pl.ds(row, 1)]
        send(r1, ea.at[pl.ds(1, 6), pl.ds(2, 8), pl.ds(row, 1)], there, (0, s, 0))
    rim(r1, ea.at[0], ex.at[0], pk, pkr)

    own1 = (iota((16, 128), 1) >= 32) & (iota((16, 128), 1) < 96)

    def scaled_terms(fields, inside):
        diag = fields[6]
        for q in range(6):
            diag = diag + fields[q]
        diag = jnp.where(inside, diag, 1.0)
        scale = jnp.where(inside, RELAX / diag, 0.0)
        return [fields[q] * scale for q in range(6)] + [jnp.where(inside, diag * (1.0 / RELAX), 0.0)]

    def pairs(q, a, b):
        pick = PICKS[q][0]
        return a + b if pick is None else (b if pick else a)

    def lanes01(pick):
        return mat(128, 128, lambda i, j: (j == 32 + (i >> 1)) & low_lanes(i, pick))

    def lanes12(pick):
        return mat(128, 128, lambda i, j: (j == 16 + (i >> 1)) & (i >= 32) & (i < 96) & low_lanes(i, pick))

    def lanes23(pick):
        return mat(128, 128, lambda i, j: (j == (i >> 1)) & (i >= 32) & (i < 64) & low_lanes(i, pick))

    def rows01(pick):
        return mat(16, 32, lambda i, j: ((j >> 3) == (i & 3)) & (((j & 7) >> 1) == (i >> 2)) & low_lanes(j, pick))

    def rows12(pz, px):
        return mat(
            8, 16,
            lambda i, j: ((j >> 3) == (i >> 1)) & (((j & 3) >> 1) == (i & 1)) & low_lanes(j, pz) & low_lanes(j >> 2, px),
        )

    def rows23(pz, px):
        return mat(8, 8, lambda i, j: (i == 0) & (j < 4) & low_lanes(j, pz) & low_lanes(j >> 1, px))

    def halves(block):
        return jnp.where(own8, block[0:8], roll(block[8:16], 64, 1))

    def zslot(k):
        return (4 - k) % 4

    def xplace(own, per, a):
        return own - per * a

    own8 = (ly >= 32) & (ly < 96)
    level1 = []
    for q in range(7):
        planes = [pairs(q, (cu[q, 2 * z] if q < 6 else r_ref[2 * z]), (cu[q, 2 * z + 1] if q < 6 else r_ref[2 * z + 1])) for z in range(4)]
        stacked = jnp.concatenate(planes, axis=0)
        level1.append(right(left(rows01(PICKS[q][1]), stacked), lanes01(PICKS[q][2])))
    scaled1 = scaled_terms(level1, own1)
    d1_own = scaled1[6]
    strip = jnp.zeros((8, 128), F32)
    for q in range(7):
        block = halves(scaled1[q])
        for x in range(2):
            p1[q, 1, x, 0:4, :] = block[4 * x : 4 * x + 4]
        if q < 6:
            for h in range(2):
                t = 4 * (2 * q + h)
                moved = roll(scaled1[q][8 * h : 8 * h + 8], t - 92, 1)
                strip = jnp.where(((ly >= t) & (ly < t + 4)) | ((ly >= t + 68) & (ly < t + 72)), moved, strip)
    for x in range(2):
        s1[x, 0:4, :] = strip[4 * x : 4 * x + 4]
    c1_copies = net.group()
    for k, a in ZX:
        n = 6 if a else 7
        there = p1.at[pl.ds(0, n), pl.ds(1 - a, 1), :, pl.ds(4 * zslot(k), 4)]
        send(c1_copies, p1.at[pl.ds(0, n), pl.ds(1, 1), :, pl.ds(0, 4)], there, (k, a, 0))
    level2 = [right(left(rows12(PICKS[q][0], PICKS[q][1]), level1[q]), lanes12(PICKS[q][2])) for q in range(7)]
    level3 = [right(left(rows23(PICKS[q][0], PICKS[q][1]), level2[q]), lanes23(PICKS[q][2])) for q in range(7)]
    inside2 = (ly >= 32) & (ly < 64) & (sx < 4)
    inside3 = (ly >= 16) & (ly < 32) & (sx < 1)
    scaled2 = scaled_terms(level2, inside2)
    scaled3 = scaled_terms(level3, inside3)
    group = [jnp.zeros((8, 128), F32), jnp.zeros((8, 128), F32)]
    line = jnp.zeros((8, 128), F32)
    for q in range(7):
        g, j = q // 4, q % 4
        group[g] = group[g] + roll(scaled2[q], 32 * j - 32, 1)
        line = line + roll(scaled3[q], 16 * q - 16, 1)
    for g in range(2):
        for x in range(2):
            a2[1, 2 * g + x, 0:2, :] = group[g][2 * x : 2 * x + 2]
    a3[1, 0:1, :] = line[0:1]
    z_copies = net.group()
    for k in range(4):
        for t in (0, 1, -1):
            if k or t:
                there = a2.at[pl.ds(1 - t, 1), :, pl.ds(2 * zslot(k), 2)]
                send(z_copies, a2.at[pl.ds(1, 1), :, pl.ds(0, 2)], there, (k, 0, t))
                send(z_copies, a3.at[pl.ds(1, 1), pl.ds(0, 1)], a3.at[pl.ds(1 - t, 1), pl.ds(zslot(k), 1)], (k, 0, t))

    rows_r1, lanes_r1 = rows01(None), lanes01(None)
    wait(r1)
    pl.semaphore_wait(go_a, 2)
    for a in (4, -4):
        net.signal(go_b, (0, a, 0))

    def unpack(pr, y, xy):
        from_low = (ly & jnp.where(ly < 32, 2, 1)) == 0

        def both(low, high):
            return jnp.where(from_low, pr[low], pr[high])

        beside = both(0, 1)
        for z in range(8):
            y[1 + z] = roll(beside, -(4 * z + 2), 1)
        y[0] = roll(both(2, 3), -30, 1)
        y[9] = roll(both(4, 5), -2, 1)
        across = jnp.where(sx < 4, both(8, 9), both(6, 7))
        for z in range(8):
            xy[z] = roll(across, -(4 * z + 2), 1)
        return beside

    beside = unpack(pkr, ey.at[0], exy)
    for q in range(6):
        for z in range(8):
            ey[1 + q, 1 + z] = roll(beside, -(32 + 16 * q + 2 * z + 1), 1)

    def sweep(here, zp, zn, xp, xn, yp, yn, rhs, s):
        total = KEEP * here + rhs
        total = total + s[0] * zn + s[1] * zp
        total = total + s[2] * xn + s[3] * xp
        return total + s[4] * yn + s[5] * yp

    def sweep_a(a, x, y, p, outer):
        here = a[p]
        bx, by = x[p - outer], y[p - outer]
        return sweep(
            here, a[p - 1], a[p + 1], xprev(here, bx), xnext(here, bx), yprev(here, by), ynext(here, by),
            ea[0, p], [ea[1 + q, p] for q in range(6)],
        )

    def rim_sweep(a, x, y, xy):
        for p in range(1, 11):
            va[p] = sweep_a(a, x, y, p, 1)
        for z in range(8):
            here = x[1 + z]
            ba, bxy = a[2 + z], xy[z]
            vx[z] = sweep(
                here, x[z], x[2 + z], xprev(here, ba), xnext(here, ba), yprev(here, bxy), ynext(here, bxy),
                ex[0, 1 + z], [ex[1 + q, 1 + z] for q in range(6)],
            )
            here = y[1 + z]
            vy[z] = sweep(
                here, y[z], y[2 + z], xprev(here, bxy), xnext(here, bxy), yprev(here, ba), ynext(here, ba),
                ey[0, 1 + z], [ey[1 + q, 1 + z] for q in range(6)],
            )

    rim_sweep(ea.at[0], ex.at[0], ey.at[0], exy)
    planes = []
    for z in range(4):
        two = [(sweep_a(va, vx, vy, 2 + p, 2) - va[2 + p]) * d0[p] for p in (2 * z, 2 * z + 1)]
        planes.append(two[0] + two[1])
    rhs1 = right(left(rows_r1, jnp.concatenate(planes, axis=0)), lanes_r1)
    rhs1 = halves(jnp.where(own1, rhs1 / jnp.where(own1, d1_own, 1.0), 0.0))
    for x in range(2):
        b1c[1, 1, x, 0:4, :] = rhs1[4 * x : 4 * x + 4]

    r2 = net.group()
    for k, a, t in NEAR_27:
        if (k, a, t) != (0, 0, 0):
            there = b1c.at[1 - t, 1 - a, :, pl.ds(4 * zslot(k), 4)]
            send(r2, b1c.at[1, 1, :, pl.ds(0, 4)], there, (k, a, t))

    pl.semaphore_wait(go_c, 2)
    for k, a in [(0, 0)] + ZX:
        for t in (1, -1):
            there = s1l if t == 1 else s1h
            send(c1_copies, s1.at[:, pl.ds(0, 4)], there.at[1 - a, :, pl.ds(4 * zslot(k), 4)], (k, a, t))

    pack = jnp.zeros((8, 128), F32)
    for z in range(8):
        plane = va[2 + z]
        wa[2 + z] = plane
        pack = jnp.where((ly >= 4 * z) & (ly < 4 * z + 4), roll(plane, 4 * z + 2, 1), pack)
    wpk[...] = pack
    up0 = net.group()
    rim(up0, wa, wx, wpk, wpkr)

    wait(z_copies)
    for q in range(7):
        g, j = q // 4, q % 4
        for x in range(2):
            low, mid, high = [roll(a2[t, 2 * g + x], 32 * t - 32 * j, 1) for t in range(3)]
            c2[q, 6 + x] = jnp.where(ly < 32, low, jnp.where(ly < 64, mid, jnp.where(ly < 96, high, 0.0)))
    c2_copies = net.group()
    for a in (1, -1, 2, -2, 3, -3):
        send(c2_copies, c2.at[pl.ds(0, 6), pl.ds(6, 2)], c2.at[pl.ds(0, 6), pl.ds(xplace(6, 2, a), 2)], (0, a, 0))
    fields3 = []
    for q in range(7):
        low, mid, high = [roll(a3[t], 16 * t - 16 * q, 1) for t in range(3)]
        fields3.append(jnp.where(ly < 16, low, jnp.where(ly < 32, mid, jnp.where(ly < 48, high, 0.0))))
    for q in range(3):
        c3[q, 0] = jnp.where(ly < 64, fields3[2 * q], roll(fields3[2 * q + 1], 64, 1))

    def sweep_l(v, b, c, x):
        here = v[x]
        return sweep(
            here, roll(here, 1, 0), roll(here, -1, 0), v[x - 1], v[x + 1], roll(here, 1, 1), roll(here, -1, 1),
            b[x], [c[q, x] for q in range(6)],
        )

    wait(c1_copies)
    lane16 = iota((16, 128), 1)
    own16 = (lane16 >= 32) & (lane16 < 96)
    for i in range(3):
        for x in range(2):
            rims = jnp.where(lane16 < 64, s1l[i, x], s1h[i, x])
            for q in range(6):
                block = p1[q, i, x]
                c1[q, 4 * i + x] = jnp.where(own16, block, roll(rims, 28 - 8 * q, 1))
                c1[q, 4 * i + 2 + x] = jnp.where(own16, roll(block, 64, 1), roll(rims, 24 - 8 * q, 1))
    for x in range(2):
        block = p1[6, 1, x]
        c1[6, 4 + x] = block
        c1[6, 6 + x] = roll(block, 64, 1)
    halve, lanes_r2 = mat(8, 16, lambda i, j: (j >> 1) == i), lanes12(None)
    wait(r2)
    for i in range(3):
        for x in range(2):
            low, mid, high = [b1c[t, i, x] for t in range(3)]
            b1[4 * i + x] = jnp.where(own16, mid, roll(jnp.where(lane16 >= 64, low, high), 64, 1))
            b1[4 * i + 2 + x] = jnp.where(own16, roll(mid, 64, 1), jnp.where(lane16 < 64, low, high))
    for x in range(1, 11):
        v1p[x] = sweep_l(b1, b1, c1, x)
    rows = []
    for x in range(2):
        two = [(sweep_l(v1p, b1, c1, p) - v1p[p]) * c1[6, p] for p in (4 + 2 * x, 5 + 2 * x)]
        rows.append(two[0] + two[1])
    rows = right(jnp.concatenate(rows, axis=0), lanes_r2)
    for x in range(2):
        inside = (ly >= 32) & (ly < 64)
        rhs2 = left(halve, rows[16 * x : 16 * x + 16])
        rhs2 = jnp.where(inside, rhs2 / jnp.where(inside, c2[6, 6 + x], 1.0), 0.0)
        b2c[6 + x] = rhs2
        b2r[x] = roll(rhs2, 32, 1) + roll(rhs2, -32, 1)

    r3 = net.group()
    for a in (3, -3, 2, -2, 1, -1, 0):
        there = pl.ds(xplace(6, 2, a), 2)
        send(r3, b2r, b2l.at[there], (0, a, 1))
        send(r3, b2r, b2h.at[there], (0, a, -1))
    for a in (3, -3, 2, -2, 1, -1):
        send(r3, b2c.at[pl.ds(6, 2)], b2c.at[pl.ds(xplace(6, 2, a), 2)], (0, a, 0))
    pl.semaphore_wait(go_b, 2)
    c3_copies = net.group()
    for a in range(1, 16):
        send(c3_copies, c3.at[:, pl.ds(0, 1), pl.ds(0, 4)], c3.at[:, pl.ds(16 - a, 1), pl.ds(0, 4)], (0, a, 0))

    wait(c2_copies)
    lanes_r3 = mat(128, 128, lambda i, j: (j == (i >> 1)) & (i < 96))
    rows_r3 = mat(8, 8, lambda i, j: (j >> 1) == (i & 3))
    wait(r3)
    for x in range(14):
        b2[x] = jnp.where(ly < 32, b2l[x], jnp.where(ly >= 64, b2h[x], b2c[x]))
    for x in range(2, 12):
        v2p[x] = sweep_l(b2, b2, c2, x)
    two = [(sweep_l(v2p, b2, c2, p) - v2p[p]) * c2[6, p] for p in (6, 7)]
    rows = right(two[0] + two[1], lanes_r3)
    rhs3 = left(rows_r3, rows)

    def twice(block):
        return jnp.where(sx < 4, block, roll(block, 4, 0))

    inside = ly < 48
    rhs3 = jnp.where(inside, rhs3 / jnp.where(inside, twice(fields3[6]), 1.0), 0.0)
    b3[0] = rhs3

    r4 = net.group()
    for a in ALONG_X:
        send(r4, b3.at[pl.ds(0, 1)], b3.at[pl.ds(16 - a, 1)], (0, a, 0))
    wait(c3_copies)
    terms3 = []
    for q in range(3):
        terms3.append([twice(c3[q, x]) for x in range(16)])
        terms3.append([roll(block, 64, 1) for block in terms3[-1]])
    def lanes10(i, j):
        main = (j < 128) & (i == 32 + (j >> 1))
        return main | ((j >= 254) & (i == 31)) | ((j >= 128) & (j < 130) & (i == 96))

    def rows10(i, j):
        xi, zr = j >> 4, j & 15
        main = (i < 96) & (zr == (((i >> 4) + 15) & 15)) & (xi == 1 + ((i & 7) >> 1))
        n = i - 96
        beside = (i >= 96) & (zr == ((((n >> 3) + 31) >> 1) & 15)) & (
            (((n & 7) >= 6) & (xi == 0)) | (((n & 7) < 2) & (xi == 5))
        )
        return main | beside

    rows_32, lanes_32 = mat(8, 8, lambda i, j: j == (i >> 1)), mat(128, 128, lambda i, j: (i == (j >> 1)) & (j < 96))
    rows_21, lanes_21 = mat(16, 8, lambda i, j: j == (i >> 1)), mat(128, 128, lambda i, j: i == 16 + (j >> 1))
    rows_10, lanes_10 = mat(176, 96, rows10), mat(128, 256, lanes10)
    wait(r4)
    rhs3 = [b3[x] for x in range(16)]
    here = rhs3
    for _ in range(7):
        here = [
            sweep(
                here[x], roll(here[x], 1, 0), roll(here[x], -1, 0), here[(x + 15) % 16], here[(x + 1) % 16],
                roll(here[x], 1, 1), roll(here[x], -1, 1), rhs3[x], [terms3[q][x] for q in range(6)],
            )
            for x in range(16)
        ]

    wide = left(rows_32, jnp.concatenate([here[(X + 16) % 16] for X in range(-2, 3)], axis=1))
    wide = jnp.concatenate([wide[:, 128 * i : 128 * i + 128] for i in range(5)], axis=0)
    wide = right(wide, lanes_32)
    for x in range(2, 12):
        i = (x >> 1) - 1
        v2p[x] = v2p[x] + wide[8 * i : 8 * i + 8]
    for x in range(3, 11):
        v2q[x] = sweep_l(v2p, b2, c2, x)
    ups = [sweep_l(v2q, b2, c2, x) for x in range(4, 10)]

    wide = right(jnp.concatenate(ups, axis=0), lanes_21)
    wide = left(rows_21, jnp.concatenate([wide[8 * i : 8 * i + 8] for i in range(6)], axis=1))
    for x in range(1, 11):
        i = x >> 1
        v1p[x] = v1p[x] + wide[:, 128 * i : 128 * i + 128]
    for x in range(2, 10):
        v1q[x] = sweep_l(v1p, b1, c1, x)
    ups = [sweep_l(v1q, b1, c1, x) for x in range(3, 9)]

    wide = right(jnp.concatenate(ups, axis=0), lanes_10)
    wide = left(rows_10, wide)
    wait(up0)
    low = (ly & 2) == 0
    beside = jnp.where(low, wpkr[0], wpkr[1])
    low_z = jnp.where(low, wpkr[2], wpkr[3])
    high_z = jnp.where(low, wpkr[4], wpkr[5])
    across = jnp.where(sx < 4, jnp.where(low, wpkr[8], wpkr[9]), jnp.where(low, wpkr[6], wpkr[7]))
    a = [wa[p] + wide[8 * p : 8 * p + 8, 0:128] for p in range(12)]
    x = [wx[p] + wide[96 + 8 * p : 104 + 8 * p, 0:128] for p in range(10)]
    y = []
    for p in range(10):
        if p == 0:
            base = roll(low_z, -30, 1)
        elif p == 9:
            base = roll(high_z, -2, 1)
        else:
            base = roll(beside, -(4 * (p - 1) + 2), 1)
        y.append(base + wide[8 * (p + 1) : 8 * (p + 1) + 8, 128:256])
    xy = [roll(across, -(4 * z + 2), 1) + wide[104 + 8 * z : 112 + 8 * z, 128:256] for z in range(8)]
    rim_sweep(a, x, y, xy)
    for z in range(8):
        out_ref[z] = sweep_a(va, vx, vy, 2 + z, 2)
    net.finish()


def on_device(source, decay_rate, dispersion, velocity, upwind):
    def vmem(*shape):
        return pltpu.VMEM(shape, F32)

    tile = (8, 128)
    scratch = [
        vmem(8, *tile), vmem(8, *tile), vmem(3, 8, *tile), vmem(3, 8, *tile), pltpu.VMEM((3, 8, *tile), jnp.int32),
        pltpu.SemaphoreType.DMA((5,)),
        vmem(3, 8, *tile), vmem(5, *tile), vmem(*tile), vmem(3, 8, *tile), vmem(3, *tile), vmem(2, *tile), vmem(*tile), vmem(*tile),
        vmem(7, 12, *tile), vmem(7, 10, *tile), vmem(7, 10, *tile), vmem(8, *tile), vmem(*tile), vmem(10, *tile),
        vmem(6, 8, *tile), vmem(8, *tile), vmem(12, *tile), vmem(8, *tile), vmem(8, *tile),
        vmem(12, *tile), vmem(10, *tile), vmem(*tile), vmem(10, *tile),
        vmem(7, 3, 2, 16, 128), vmem(2, *tile), vmem(3, 2, 16, 128), vmem(3, 2, 16, 128), vmem(3, 4, *tile), vmem(3, *tile),
        vmem(7, 12, 16, 128), vmem(7, 14, *tile), vmem(3, 16, *tile),
        vmem(3, 3, 2, 16, 128), vmem(12, 16, 128), vmem(12, 16, 128), vmem(12, 16, 128),
        vmem(14, *tile), vmem(2, *tile), vmem(14, *tile), vmem(14, *tile), vmem(14, *tile), vmem(14, *tile), vmem(14, *tile),
        vmem(16, *tile),
        pltpu.SemaphoreType.REGULAR, pltpu.SemaphoreType.REGULAR, pltpu.SemaphoreType.REGULAR,
        vmem(768, 128), pltpu.SemaphoreType.DMA((GROUPS,)), pltpu.SemaphoreType.DMA((GROUPS,)),
    ]
    return pl.pallas_call(
        kernel,
        out_shape=jax.ShapeDtypeStruct((8, 8, 128), F32),
        in_specs=[pl.BlockSpec(memory_space=pltpu.HBM)] * 5,
        out_specs=pl.BlockSpec(memory_space=pltpu.VMEM),
        scratch_shapes=scratch,
        compiler_params=pltpu.CompilerParams(collective_id=0, has_side_effects=True),
    )(source, decay_rate, dispersion, velocity, upwind)


def solution(mesh):
    field, vector = P("gz", "gx", "gy"), P(None, "gz", "gx", "gy")
    return jax.shard_map(
        on_device, mesh=mesh, in_specs=(field, field, vector, vector, vector), out_specs=field, check_vma=False
    )
```
